32 devices in a mesh: parts: 2 (over y), node: 4 (over x, core), local: 4 (over z).
Axes of the slice: x: 2, y: 2, z: 4, core: 2. Of those that a mesh axis runs over, the one named last changes fastest.
Arguments:
- tokens: bfloat16 [2048, 7168], P(('parts', 'node', 'local')), parts along dimension 0, may hold values from -6 to 6
- expert_ids: int32 [2048, 2], P(('parts', 'node', 'local')), parts along dimension 0, may hold values from 0 to 31, all different within a row; in each aligned block of 64 rows (0 to 63, 64 to 127, ...) at most 5 rows name the same one
- gate_weights: float32 [2048, 2], P(('parts', 'node', 'local')), parts along dimension 0, may hold values from 0.1 to 1
- w_gate: bfloat16 [32, 7168, 1024], P('local', None, 'node'), may hold values from -0.0625 to 0.0625
- w_up: bfloat16 [32, 7168, 1024], P('local', None, 'node'), may hold values from -0.0625 to 0.0625
- w_down: bfloat16 [32, 1024, 7168], P('local', 'node'), may hold values from -0.1875 to 0.1875
Outputs:
- mixed: bfloat16 [2048, 7168], P(('parts', 'node', 'local')), parts along dimension 0
The draws below stay inside these ranges and needn't reach their ends.
There are 2 independent parts, one for each index of `parts`. The reference program is written for one: setup_inputs(seed, part) draws one part's arguments, and reference() takes and returns one part's arrays. A program takes and returns all parts, laid end to end along the dimension named above; an argument that names none is the same for every part. Nothing has to cross between parts.
Inputs may be any that keep to these rules, and one draw needn't show every extreme that they name: `expert_ids`: A row names 2 different experts. In each aligned block of 64 rows (the tokens of one device) no expert is named by more than 5 rows, a bound that some block reaches.
All inputs are finite; a program needn't handle non-finite values.
Results may differ from the reference program's by a relative error of at most 0.012.
Values may be sent and summed in bfloat16 or wider, within the bound.
No kernel may reach another device: no remote copies, remote signals or barrier semaphores. Data moves between devices by JAX's collectives and lax.ppermute only.
A program may use at most 256 MiB of HBM per device.

```python
import math
import jax
import jax.numpy as jnp
import numpy as np
from jax import lax

D = 7168
FF = 1024
EXPERTS = 32
TOPK = 2
TOK_DEV = 64
CAP = 5
TOKENS = 1024
N_NODE = 4


def level_of(rng, extent, cuts, smallest, top_value):
    loudness = 1.0
    for dim, blocks in cuts:
        steps = jax.random.uniform(jax.random.fold_in(jax.random.fold_in(rng, 6), dim), (blocks,), jnp.float32, smallest / len(cuts), top_value / len(cuts))
        loudness = loudness * jnp.repeat(jnp.exp(steps), extent[dim] // blocks).reshape((-1,) + (1,) * (len(extent) - 1 - dim))
    return loudness


def routed_block(stream_key, own, number, rows, count, top, most, lean):
    ranking = jax.random.permutation(stream_key, count)
    packed, ordinary = load_shares(count, rows * top, most, lean, True), load_shares(count, rows * top, most, lean, False)
    places = jnp.arange(count)

    def named(lengths, offset_by):
        used = int((lengths > 0).sum())
        fixed = max(1, used // 4)
        passed = fixed + (places - fixed + offset_by * (used - fixed)) % max(1, count - fixed)
        return jnp.zeros((count,), jnp.int32).at[ranking[jnp.where(places < fixed, places, passed)]].set(jnp.asarray(lengths, jnp.int32))

    lengths = jnp.where(number % 4 == 0, named(packed, number // 4), named(ordinary, number - number // 4 - 1))
    mixed = jax.random.permutation(jax.random.fold_in(own, 3), count)
    giver, sink = mixed[0:count // 2 * 2:2], mixed[1:count // 2 * 2:2]
    margin = jnp.minimum(lengths[giver] - 1, most - lengths[sink]) // 2
    margin = jnp.where((giver == ranking[0]) | (sink == ranking[0]) | (lengths[sink] == 0), 0, jnp.maximum(margin, 0))
    passed = jax.random.randint(jax.random.fold_in(own, 4), (count // 2,), 0, 1 << 20) % (margin + 1)
    lengths = lengths.at[giver].add(-passed).at[sink].add(passed)
    labels = jnp.searchsorted(jnp.cumsum(lengths), jnp.arange(rows * top), side="right").astype(jnp.int32)
    listing = labels.reshape(top, rows).T
    listing = listing[jax.random.permutation(jax.random.fold_in(own, 1), rows)]
    offset_by = jax.random.randint(jax.random.fold_in(own, 2), (rows, 1), 0, top)
    return jnp.take_along_axis(listing, (jnp.arange(top)[None, :] + offset_by) % top, axis=1)


def load_shares(amount, total, most, skew, full):
    weights = [(1 << 20) // math.isqrt(grade ** skew) + 1 for grade in range(1, amount + 1)]
    largest = most if full else min(most, max(-(-total // amount), total * weights[0] // sum(weights)))
    least = 1 if total - largest >= amount - 1 else 0
    given, surplus = [largest] + [least] * (amount - 1), total - largest - least * (amount - 1)
    while surplus > 0:
        movable = [i for i in range(1, amount) if given[i] < largest] or [i for i in range(1, amount) if given[i] < most]
        mass, budget = sum([weights[i] for i in movable]), surplus
        for i in movable:
            addition = min(most - given[i], max(1, budget * weights[i] // mass), surplus)
            given[i] = given[i] + addition
            surplus = surplus - addition
    return np.array(given)


def normal_values(stream_key, shape, width, reach, cuts=(), held_as=jnp.bfloat16):
    array = jax.random.normal(stream_key, shape, jnp.float32) * width
    if len(cuts) > 0:
        array = level_of(stream_key, shape, cuts, -0.22, 0.18) * array
    return jnp.clip(array, min=-reach, max=reach).astype(held_as)


def setup_inputs(seed: int = 0, part: int = 0) -> dict:
    key_of = jax.random.split(jax.random.key(seed), 7)
    own_keys = jax.random.split(jax.random.fold_in(key_of[6], part), 7)
    tokens = normal_values(own_keys[0], (TOKENS, D), 1.0, 6.0, ((0, 16),))
    expert_ids_keys = jax.random.split(jax.random.fold_in(own_keys[1], 1), TOKENS // TOK_DEV)
    expert_ids_turns = jax.random.permutation(jax.random.fold_in(own_keys[1], 3), TOKENS // TOK_DEV)
    expert_ids = jax.vmap(lambda own, number: routed_block(jax.random.fold_in(own_keys[1], 2), own, number, TOK_DEV, EXPERTS, TOPK, CAP, 2))(expert_ids_keys, expert_ids_turns).reshape((TOKENS, TOPK))
    gate_weights = jnp.clip(0.1 + 0.9 * jax.random.uniform(own_keys[2], (TOKENS, TOPK), jnp.float32) ** level_of(own_keys[2], (TOKENS, TOPK), ((0, 16),), -0.2, 0.2), 0.1, 1.0)
    w_gate = normal_values(key_of[3], (EXPERTS, D, FF), D ** -0.5, 0.0625, ((0, 4), (2, 4)))
    w_up = normal_values(key_of[4], (EXPERTS, D, FF), D ** -0.5, 0.0625, ((0, 4), (2, 4)))
    w_down = normal_values(key_of[5], (EXPERTS, FF, D), FF ** -0.5, 0.1875, ((0, 4), (1, 4)))
    return {"tokens": tokens, "expert_ids": expert_ids, "gate_weights": gate_weights, "w_gate": w_gate, "w_up": w_up, "w_down": w_down}


def block_slots(id_block):
    pair_ids = id_block.reshape(-1)
    onehot = (pair_ids[:, None] == jnp.arange(EXPERTS, dtype=jnp.int32)[None, :]).astype(jnp.int32)
    running = jnp.cumsum(onehot, axis=0)
    return jnp.sum(running * onehot, axis=1) - 1


def reference(tokens, expert_ids, gate_weights, w_gate, w_up, w_down):
    blocks = TOKENS // TOK_DEV
    slot_of = jax.vmap(block_slots)(expert_ids.reshape(blocks, TOK_DEV, TOPK))
    block_index = jnp.arange(blocks, dtype=jnp.int32)[:, None]
    flat_ids = expert_ids.reshape(blocks, TOK_DEV * TOPK)
    target = ((flat_ids * blocks + block_index) * CAP + slot_of).reshape(-1).astype(jnp.int32)
    token_index = jnp.repeat(jnp.arange(TOKENS, dtype=jnp.int32), TOPK)
    table_size = EXPERTS * blocks * CAP
    owner_row = jnp.full((table_size,), TOKENS, jnp.int32).at[target].set(token_index)
    weight = jnp.zeros((table_size,), jnp.float32).at[target].set(gate_weights.reshape(-1))
    owner_row = owner_row.reshape(EXPERTS, blocks * CAP)
    weight = weight.reshape(EXPERTS, blocks * CAP)
    padded = jnp.concatenate([tokens, jnp.zeros((1, D), tokens.dtype)], axis=0)

    def one_expert(summed, inputs):
        rows_owner, rows_weight, gate_mat, up_mat, down_mat = inputs
        picked = jnp.take(padded, rows_owner, axis=0)
        gate_part = jnp.dot(picked, gate_mat, preferred_element_type=jnp.float32)
        up_part = jnp.dot(picked, up_mat, preferred_element_type=jnp.float32)
        hidden = (jax.nn.silu(gate_part) * up_part).astype(jnp.bfloat16)
        quarters = hidden.reshape(-1, N_NODE, FF // N_NODE).astype(jnp.float32)
        down_part = down_mat.reshape(N_NODE, FF // N_NODE, D).astype(jnp.float32)
        pieces = jnp.einsum("mqf,qfd->qmd", quarters, down_part, precision=lax.Precision.HIGHEST).astype(jnp.bfloat16)
        pieces = lax.optimization_barrier(pieces)
        added = jnp.sum(pieces.astype(jnp.float32), axis=0)
        return summed.at[rows_owner].add(rows_weight[:, None] * added), None

    summed = jnp.zeros((TOKENS + 1, D), jnp.float32)
    summed, _ = lax.scan(one_expert, summed, (owner_row, weight, w_gate, w_up, w_down))
    return summed[:TOKENS].astype(jnp.bfloat16)
```

```python
import functools

import jax
import jax.numpy as jnp
import numpy as np
from jax import lax
from jax.experimental import pallas as pl
from jax.experimental.pallas import tpu as pltpu
from jax.sharding import PartitionSpec as P

CAP = 5
CHUNKS = 4
VMEM_LIMIT = 56 * 1024 * 1024
F32, BF16 = jnp.float32, jnp.bfloat16


def pad16(n):
    return -(-n // 16) * 16


def params():
    return pltpu.CompilerParams(vmem_limit_bytes=VMEM_LIMIT)


def whole():
    return pl.BlockSpec(memory_space=pltpu.VMEM)


class Sizes:
    def __init__(self, tokens, w_gate, local_count, node_count):
        self.tok, self.width = tokens.shape
        self.exp_dev = w_gate.shape[0]
        self.hidden = w_gate.shape[2]
        self.local = local_count
        self.node = node_count
        self.R = self.exp_dev * CAP
        self.RP = pad16(self.R)
        self.MP = pad16(self.local * CAP)
        self.rows = self.local * self.RP
        self.grouped = self.exp_dev * self.MP
        self.relative = local_count <= 4
        self.groups = [1] * local_count if self.relative else [local_count]
        self.chunks = CHUNKS
        self.dc = self.width // self.chunks

    def columns(self):
        table = np.full((8, self.rows), -1, np.int32)
        for s in range(self.local):
            for q in range(self.R):
                table[:3, s * self.RP + q] = (s, q // CAP, q % CAP)
            table[0, s * self.RP : (s + 1) * self.RP] = s
        return table

    def regroup(self):
        m = np.zeros((self.grouped, self.rows), np.float32)
        for s in range(self.local):
            for j in range(self.exp_dev):
                for c in range(CAP):
                    m[j * self.MP + s * CAP + c, s * self.RP + j * CAP + c] = 1
        return m


def gather_kernel(z, plane_ref, table_ref, ids_ref, gates_ref, tokens_ref, weight_ref, *outs):
    block, expert, slot = (table_ref[i : i + 1, :] for i in range(3))
    plane = block
    if z.relative:
        plane = block + plane_ref[0]
        plane = jnp.where(plane >= z.local, plane - z.local, plane)
    name = jnp.where(slot >= 0, plane * z.exp_dev + expert, -1)
    ids, gates = ids_ref[...], gates_ref[...]
    top = ids.shape[1]
    hits = [ids[:, k : k + 1] == name for k in range(top)]
    named = hits[0].astype(F32)
    for k in range(1, top):
        named = named + hits[k].astype(F32)
    t0 = lax.broadcasted_iota(jnp.int32, (z.tok, z.tok), 0)
    t1 = lax.broadcasted_iota(jnp.int32, (z.tok, z.tok), 1)
    before = jnp.where(t1 < t0, 1.0, 0.0).astype(BF16)
    rank = jnp.dot(before, named.astype(BF16), preferred_element_type=F32)
    here = rank == slot.astype(F32)
    weight = jnp.zeros((z.tok, z.rows), F32)
    for k in range(top):
        weight = weight + jnp.where(hits[k] & here, gates[:, k : k + 1], 0.0)
    weight_ref[...] = weight
    pick = jnp.where(here, named, 0.0).T.astype(BF16)
    at = 0
    for c in range(z.chunks):
        cols = slice(c * z.dc, (c + 1) * z.dc)
        picked = jnp.dot(pick, tokens_ref[:, cols], preferred_element_type=F32).astype(BF16)
        s = 0
        for g in z.groups:
            for i in range(g):
                outs[at][i] = picked[s * z.RP : s * z.RP + z.R]
                s += 1
            at += 1


def gather_rows(z, plane, ids, gates, tokens):
    shapes = [jax.ShapeDtypeStruct((g, z.R, z.dc), BF16) for _ in range(z.chunks) for g in z.groups]
    outs = pl.pallas_call(
        functools.partial(gather_kernel, z),
        out_shape=[jax.ShapeDtypeStruct((z.tok, z.rows), F32)] + shapes,
        in_specs=[pl.BlockSpec(memory_space=pltpu.SMEM)] + [whole()] * 4,
        out_specs=[whole()] * (1 + len(shapes)),
        compiler_params=params(),
        name="gather_rows",
    )(plane, jnp.asarray(z.columns()), ids, gates, tokens)
    n = len(z.groups)
    return outs[0], [outs[1 + c * n : 1 + (c + 1) * n] for c in range(z.chunks)]


def tile_of(width):
    for t in (512, 256, 128):
        if width % t == 0:
            return t
    return width


def up_kernel(z, counts, first, last, *refs):
    pieces = refs[: len(counts)]
    refs = refs[len(counts) :]
    regroup_ref, wg_ref, wu_ref = refs[:3]
    refs = refs[3:]
    if not first:
        gin_ref, uin_ref = refs[:2]
        refs = refs[2:]
    if last:
        hidden_ref, rows_ref, grouped_ref = refs
    else:
        gout_ref, uout_ref, rows_ref, grouped_ref = refs

    @pl.when(pl.program_id(0) == 0)
    def _():
        if z.RP > z.R:
            rows_ref[...] = jnp.zeros_like(rows_ref)
        at = 0
        for ref, count in zip(pieces, counts):
            for i in range(count):
                m, s = divmod(at, z.local)
                rows_ref[m, s * z.RP : s * z.RP + z.R, :] = ref[i]
                at += 1
        tile = tile_of(z.dc)

        def step(i, carry):
            cols = pl.ds(pl.multiple_of(i * tile, tile), tile)
            for m in range(z.node):
                got = jnp.dot(regroup_ref[...], rows_ref[m, :, cols], preferred_element_type=F32).astype(BF16)
                grouped_ref[:, m * z.MP : (m + 1) * z.MP, cols] = got.reshape(z.exp_dev, z.MP, tile)
            return carry

        lax.fori_loop(0, z.dc // tile, step, 0)

    rows = grouped_ref[pl.program_id(0)]
    gate = jnp.dot(rows, wg_ref[0], preferred_element_type=F32)
    up = jnp.dot(rows, wu_ref[0], preferred_element_type=F32)
    if not first:
        gate = gate + gin_ref[0]
        up = up + uin_ref[0]
    if last:
        hidden_ref[0] = (gate / (1.0 + jnp.exp(-gate)) * up).astype(BF16)
    else:
        gout_ref[0] = gate
        uout_ref[0] = up


def up_chunk(z, c, pieces, regroup, w_gate, w_up, sums):
    first, last = sums is None, c == z.chunks - 1
    counts = [p.shape[0] for p in pieces]
    acc = jax.ShapeDtypeStruct((z.exp_dev, z.node * z.MP, z.hidden), F32)
    acc_spec = pl.BlockSpec((1,) + acc.shape[1:], lambda e: (e, 0, 0))
    w_spec = pl.BlockSpec((1, z.dc, z.hidden), lambda e: (e, c, 0))
    out_shape = [jax.ShapeDtypeStruct(acc.shape, BF16)] if last else [acc, acc]
    flops = 4 * z.exp_dev * z.node * z.MP * z.dc * z.hidden
    return pl.pallas_call(
        functools.partial(up_kernel, z, counts, first, last),
        grid=(z.exp_dev,),
        out_shape=out_shape,
        in_specs=[pl.BlockSpec(p.shape, lambda e: (0, 0, 0)) for p in pieces]
        + [pl.BlockSpec(regroup.shape, lambda e: (0, 0)), w_spec, w_spec]
        + ([] if first else [acc_spec, acc_spec]),
        out_specs=[acc_spec] * len(out_shape),
        scratch_shapes=[
            pltpu.VMEM((z.node, z.rows, z.dc), BF16),
            pltpu.VMEM((z.exp_dev, z.node * z.MP, z.dc), BF16),
        ],
        compiler_params=params(),
        cost_estimate=pl.CostEstimate(
            flops=flops, bytes_accessed=4 * z.exp_dev * z.dc * z.hidden, transcendentals=0
        ),
        name="up_chunk",
    )(*pieces, regroup, w_gate, w_up, *(() if first else sums))


def down_kernel(z, order, hidden_ref, ungroup_ref, wd_ref, *refs):
    outs, held_ref = refs[:-1], refs[-1]
    e = pl.program_id(0)
    got = jnp.dot(hidden_ref[0], wd_ref[0], preferred_element_type=F32).astype(BF16)
    for m in range(z.node):
        held_ref[m, pl.ds(pl.multiple_of(e * z.MP, z.MP), z.MP), :] = got[m * z.MP : (m + 1) * z.MP]

    @pl.when(e == z.exp_dev - 1)
    def _():
        tile = tile_of(z.dc)

        def step(i, carry):
            cols = pl.ds(pl.multiple_of(i * tile, tile), tile)
            for out, ms in zip(outs, order):
                for k, m in enumerate(ms):
                    back = jnp.dot(ungroup_ref[...], held_ref[m, :, cols], preferred_element_type=F32).astype(BF16)
                    for s in range(z.local):
                        out[k * z.local + s, :, cols] = back[s * z.RP : s * z.RP + z.R]
            return carry

        lax.fori_loop(0, z.dc // tile, step, 0)


def down_chunk(z, c, hidden, ungroup, w_down, order):
    shapes = [jax.ShapeDtypeStruct((len(ms) * z.local, z.R, z.dc), BF16) for ms in order]
    return pl.pallas_call(
        functools.partial(down_kernel, z, order),
        grid=(z.exp_dev,),
        out_shape=shapes,
        in_specs=[
            pl.BlockSpec((1,) + hidden.shape[1:], lambda e: (e, 0, 0)),
            pl.BlockSpec(ungroup.shape, lambda e: (0, 0)),
            pl.BlockSpec((1, z.hidden, z.dc), lambda e: (e, 0, c)),
        ],
        out_specs=[pl.BlockSpec(s.shape, lambda e: (0, 0, 0)) for s in shapes],
        scratch_shapes=[pltpu.VMEM((z.node, z.grouped, z.dc), BF16)],
        compiler_params=params(),
        cost_estimate=pl.CostEstimate(
            flops=2 * z.exp_dev * z.node * z.MP * z.dc * z.hidden,
            bytes_accessed=2 * z.exp_dev * z.dc * z.hidden,
            transcendentals=0,
        ),
        name="down_chunk",
    )(hidden, ungroup, w_down)


def add_kernel(cuts, a_ref, b_ref, *outs):
    for out, (lo, hi) in zip(outs, cuts):
        out[...] = (a_ref[lo:hi].astype(F32) + b_ref[lo:hi].astype(F32)).astype(BF16)


def add_cut(a, b, cuts):
    return pl.pallas_call(
        functools.partial(add_kernel, cuts),
        out_shape=[jax.ShapeDtypeStruct((hi - lo,) + a.shape[1:], BF16) for lo, hi in cuts],
        in_specs=[whole()] * 2,
        out_specs=[whole()] * len(cuts),
        compiler_params=params(),
        cost_estimate=pl.CostEstimate(flops=a.size, bytes_accessed=6 * a.size, transcendentals=0),
        name="add_cut",
    )(a, b)


def combine_kernel(z, counts, weight_ref, *refs):
    pieces, (out_ref, rows_ref) = refs[: len(counts)], refs[-2:]
    if z.RP > z.R:
        rows_ref[...] = jnp.zeros_like(rows_ref)
    at = 0
    for ref, count in zip(pieces, counts):
        for i in range(count):
            rows_ref[at * z.RP : at * z.RP + z.R, :] = ref[i]
            at += 1
    weight = weight_ref[...]
    high = weight.astype(BF16)
    rest = weight - high.astype(F32)
    middle = rest.astype(BF16)
    low = (rest - middle.astype(F32)).astype(BF16)
    rows = rows_ref[...]
    total = jnp.dot(low, rows, preferred_element_type=F32)
    total = total + jnp.dot(middle, rows, preferred_element_type=F32)
    total = total + jnp.dot(high, rows, preferred_element_type=F32)
    out_ref[...] = total.astype(BF16)


def combine_chunk(z, c, weight, pieces, so_far):
    counts = [p.shape[0] for p in pieces]
    extra = [] if so_far is None else [so_far]
    return pl.pallas_call(
        functools.partial(combine_kernel, z, counts),
        grid=(1,),
        out_shape=jax.ShapeDtypeStruct((z.tok, z.width), BF16),
        in_specs=[pl.BlockSpec(weight.shape, lambda i: (0, 0))]
        + [pl.BlockSpec(p.shape, lambda i: (0, 0, 0)) for p in pieces]
        + [pl.BlockSpec(memory_space=pl.ANY)] * len(extra),
        out_specs=pl.BlockSpec((z.tok, z.dc), lambda i: (0, c)),
        scratch_shapes=[pltpu.VMEM((z.rows, z.dc), BF16)],
        input_output_aliases={1 + len(pieces): 0} if extra else {},
        compiler_params=params(),
        name="combine_chunk",
    )(weight, *pieces, *extra)


def swap(a, mask, count):
    return lax.ppermute(a, "node", [(i, i ^ mask) for i in range(count)])


def shift(a, by, count):
    return lax.ppermute(a, "local", [(i, (i + by) % count) for i in range(count)])


def per_device(tokens, expert_ids, gate_weights, w_gate, w_up, w_down):
    local_count, node_count = lax.axis_size("local"), lax.axis_size("node")
    z = Sizes(tokens, w_gate, local_count, node_count)
    plane = lax.axis_index("local").astype(jnp.int32).reshape(1)
    regroup = z.regroup()
    ungroup = jnp.asarray(regroup.T, BF16)
    regroup = jnp.asarray(regroup, BF16)
    weight, sent = gather_rows(z, plane, expert_ids, gate_weights, tokens)

    masks = []
    while 1 << len(masks) < node_count:
        masks.append(1 << len(masks))

    sums = None
    for c in range(z.chunks):
        if z.relative:
            parts = [sent[c][0]] + [shift(sent[c][s], s, local_count) for s in range(1, local_count)]
            held = {0: [parts[0], jnp.concatenate(parts[1:], axis=0)]}
        else:
            held = {0: [lax.all_to_all(sent[c][0], "local", 0, 0, tiled=True)]}
        for mask in reversed(masks):
            for m in list(held):
                held[m | mask] = [swap(a, mask, node_count) for a in held[m]]
        pieces = [a for m in range(node_count) for a in held[m]]
        sums = up_chunk(z, c, pieces, regroup, w_gate, w_up, sums)
    hidden = sums[0]

    out = None
    for c in range(z.chunks):
        away = [m for m in range(node_count) if m & 1]
        home = [m for m in range(node_count) if not m & 1]
        send, keep = down_chunk(z, c, hidden, ungroup, w_down, [away, home])
        for mask in masks:
            got = swap(send, mask, node_count)
            half = keep.shape[0] // 2
            if mask != masks[-1]:
                nxt = mask << 1
                kept = [m for m in range(node_count) if not m & (nxt - 1)]
                cuts = [(i * local_count, (i + 1) * local_count) for i in range(len(kept))]
                if len(kept) == 2:
                    keep, send = add_cut(keep, got, cuts)
                else:
                    whole_sum = add_cut(keep, got, cuts)
                    keep = jnp.concatenate([a for a, m in zip(whole_sum, kept) if not m & nxt], axis=0)
                    send = jnp.concatenate([a for a, m in zip(whole_sum, kept) if m & nxt], axis=0)
            elif z.relative:
                pieces = add_cut(keep, got, [(s, s + 1) for s in range(local_count)])
            else:
                pieces = add_cut(keep, got, [(0, local_count)])
        if z.relative:
            pieces = [pieces[0]] + [shift(pieces[s], -s, local_count) for s in range(1, local_count)]
        else:
            pieces = [lax.all_to_all(pieces[0], "local", 0, 0, tiled=True)]
        out = combine_chunk(z, c, weight, pieces, out)
    return out


def solution(mesh):
    return jax.shard_map(
        per_device,
        mesh=mesh,
        in_specs=(
            P(("parts", "node", "local"), None),
            P(("parts", "node", "local"), None),
            P(("parts", "node", "local"), None),
            P("local", None, "node"),
            P("local", None, "node"),
            P("local", "node", None),
        ),
        out_specs=P(("parts", "node", "local"), None),
        check_vma=False,
    )
```

```python
import functools

import jax
import jax.numpy as jnp
import numpy as np
from jax import lax
from jax.experimental import pallas as pl
from jax.experimental.pallas import tpu as pltpu
from jax.sharding import PartitionSpec as P

CAP = 5
UP_PARTS = (1, 1, 1, 1)
DOWN_PARTS = (1, 1, 1, 1)
MIB = 1024 * 1024
F32, BF16 = jnp.float32, jnp.bfloat16


def pad16(n):
    return -(-n // 16) * 16


def params(mib):
    return pltpu.CompilerParams(vmem_limit_bytes=mib * MIB)


def in_vmem():
    return pl.BlockSpec(memory_space=pltpu.VMEM)


def in_hbm():
    return pl.BlockSpec(memory_space=pl.ANY)


def tie(a, *after):
    return lax.optimization_barrier((a,) + after)[0]


def cut(width, parts):
    unit = width // sum(parts)
    edges = [sum(parts[:i]) * unit for i in range(len(parts) + 1)]
    return list(zip(edges[:-1], [b - a for a, b in zip(edges[:-1], edges[1:])]))


def tile_of(width):
    for t in (512, 256, 128):
        if width % t == 0:
            return t
    return width


class Sizes:
    def __init__(self, tokens, w_gate, local_count, node_count):
        self.tok, self.width = tokens.shape
        self.exp_dev = w_gate.shape[0]
        self.hidden = w_gate.shape[2]
        self.local = local_count
        self.node = node_count
        self.R = self.exp_dev * CAP
        self.RP = pad16(self.R)
        self.MP = pad16(self.local * CAP)
        self.rows = self.local * self.RP
        self.grouped = self.exp_dev * self.MP
        self.relative = local_count <= 4
        self.up = cut(self.width, UP_PARTS)
        self.down = cut(self.width, DOWN_PARTS)

    def columns(self):
        table = np.full((self.rows, 4), -1, np.int32)
        for s in range(self.local):
            table[s * self.RP : (s + 1) * self.RP, 0] = s
            for q in range(self.R):
                table[s * self.RP + q, 1:3] = (q // CAP, q % CAP)
        return table

    def regroup(self):
        m = np.zeros((self.grouped, self.rows), np.float32)
        for s in range(self.local):
            for j in range(self.exp_dev):
                for c in range(CAP):
                    m[j * self.MP + s * CAP + c, s * self.RP + j * CAP + c] = 1
        return m


def gather_kernel(z, plan, plane_ref, table_ref, ids_ref, gates_ref, tokens_ref, weight_ref, *outs):
    block, expert, slot = (table_ref[:, i : i + 1] for i in range(3))
    plane = block
    if z.relative:
        plane = block + plane_ref[0]
        plane = jnp.where(plane >= z.local, plane - z.local, plane)
    name = jnp.where(slot >= 0, plane * z.exp_dev + expert, -1)
    ids, gates = ids_ref[...], gates_ref[...]
    top = ids.shape[0]
    hits = [ids[k : k + 1, :] == name for k in range(top)]
    named = hits[0].astype(F32)
    for k in range(1, top):
        named = named + hits[k].astype(F32)
    t0 = lax.broadcasted_iota(jnp.int32, (z.tok, z.tok), 0)
    t1 = lax.broadcasted_iota(jnp.int32, (z.tok, z.tok), 1)
    before = jnp.where(t0 < t1, 1.0, 0.0).astype(BF16)
    rank = jnp.dot(named.astype(BF16), before, preferred_element_type=F32)
    here = rank == slot.astype(F32)
    weight = jnp.zeros((z.rows, z.tok), F32)
    for k in range(top):
        weight = weight + jnp.where(hits[k] & here, gates[k : k + 1, :], 0.0)
    weight_ref[...] = weight
    pick = jnp.where(here, named, 0.0).astype(BF16)
    for lo, size, targets in plan:
        picked = jnp.dot(pick, tokens_ref[:, lo : lo + size], preferred_element_type=F32).astype(BF16)
        for s, (out, i, at) in enumerate(targets):
            outs[out][i, :, at : at + size] = picked[s * z.RP : s * z.RP + z.R]


def gather_rows(z, plane, ids, gates, tokens):
    shapes, plan = [], []
    if z.relative:
        shapes.append((1, z.R, z.width))
    for lo, size in z.up:
        if z.relative:
            n = len(shapes)
            shapes += [(1, z.R, size)] * (z.local - 1)
            targets = [(0, 0, lo)] + [(n + s, 0, 0) for s in range(z.local - 1)]
        else:
            targets = [(len(shapes), s, 0) for s in range(z.local)]
            shapes.append((z.local, z.R, size))
        plan.append((lo, size, targets))
    outs = pl.pallas_call(
        functools.partial(gather_kernel, z, plan),
        out_shape=[jax.ShapeDtypeStruct((z.rows, z.tok), F32)] + [jax.ShapeDtypeStruct(s, BF16) for s in shapes],
        in_specs=[pl.BlockSpec(memory_space=pltpu.SMEM)] + [in_vmem()] * 4,
        out_specs=[in_vmem()] * (1 + len(shapes)),
        compiler_params=params(32),
        name="gather_rows",
    )(plane, jnp.asarray(z.columns()), ids.T, gates.T, tokens)
    weight, outs = outs[0], list(outs[1:])
    own = outs.pop(0) if z.relative else None
    each = z.local - 1 if z.relative else 1
    return weight, own, [outs[i * each : (i + 1) * each] for i in range(len(z.up))]


def up_kernel(z, lo, size, counts, first, last, *refs):
    pieces = refs[: len(counts)]
    regroup_ref, wg_ref, wu_ref = refs[len(counts) : len(counts) + 3]
    refs = refs[len(counts) + 3 :]
    if not first:
        gin_ref, uin_ref = refs[:2]
        refs = refs[2:]
    if last:
        hidden_ref = refs[0]
        refs = refs[1:]
    else:
        gout_ref, uout_ref = refs[:2]
        refs = refs[2:]
    piece_ref, gate_ref, up_ref, rows_ref, grouped_ref, psem, gsem, usem = refs

    moves, at = [], 0
    for i, (ref, (count, whole)) in enumerate(zip(pieces, counts)):
        src = ref.at[:, :, pl.ds(lo, size)] if whole else ref
        moves.append(pltpu.make_async_copy(src, piece_ref.at[pl.ds(at, count)], psem.at[i]))
        at += count
    for move in moves:
        move.start()

    def weights(e):
        return (
            pltpu.make_async_copy(wg_ref.at[e, pl.ds(lo, size)], gate_ref.at[e], gsem.at[e]),
            pltpu.make_async_copy(wu_ref.at[e, pl.ds(lo, size)], up_ref.at[e], usem.at[e]),
        )

    for e in range(z.exp_dev):
        for move in weights(e):
            move.start()
    if z.RP > z.R:
        rows_ref[...] = jnp.zeros_like(rows_ref)
    tile = tile_of(size)
    at, moved = 0, 0
    for m in range(z.node):
        while at < (m + 1) * z.local:
            moves[moved].wait()
            count = counts[moved][0]
            for i in range(count):
                s = at - m * z.local
                rows_ref[m, s * z.RP : s * z.RP + z.R, :] = piece_ref[at]
                at += 1
            moved += 1

        def step(i, carry, m=m):
            cols = pl.ds(pl.multiple_of(i * tile, tile), tile)
            got = jnp.dot(regroup_ref[...], rows_ref[m, :, cols], preferred_element_type=F32).astype(BF16)
            grouped_ref[:, m * z.MP : (m + 1) * z.MP, cols] = got.reshape(z.exp_dev, z.MP, tile)
            return carry

        lax.fori_loop(0, size // tile, step, 0)

    def expert(e, carry):
        for move in weights(e):
            move.wait()
        rows = grouped_ref[e]
        gate = jnp.dot(rows, gate_ref[e], preferred_element_type=F32)
        up = jnp.dot(rows, up_ref[e], preferred_element_type=F32)
        if not first:
            gate = gate + gin_ref[e]
            up = up + uin_ref[e]
        if last:
            hidden_ref[e] = (gate / (1.0 + jnp.exp(-gate)) * up).astype(BF16)
        else:
            gout_ref[e] = gate
            uout_ref[e] = up
        return carry

    lax.fori_loop(0, z.exp_dev, expert, 0)


def up_chunk(z, c, pieces, regroup, w_gate, w_up, sums):
    lo, size = z.up[c]
    first, last = sums is None, c == len(z.up) - 1
    counts = [(p.shape[0], p.shape[2] != size) for p in pieces]
    acc = jax.ShapeDtypeStruct((z.exp_dev, z.node * z.MP, z.hidden), F32)
    out_shape = [jax.ShapeDtypeStruct(acc.shape, BF16)] if last else [acc, acc]
    return pl.pallas_call(
        functools.partial(up_kernel, z, lo, size, counts, first, last),
        out_shape=out_shape,
        in_specs=[in_hbm()] * len(pieces) + [in_vmem(), in_hbm(), in_hbm()] + ([] if first else [in_vmem()] * 2),
        out_specs=[in_vmem()] * len(out_shape),
        scratch_shapes=[
            pltpu.VMEM((z.node * z.local, z.R, size), BF16),
            pltpu.VMEM((z.exp_dev, size, z.hidden), BF16),
            pltpu.VMEM((z.exp_dev, size, z.hidden), BF16),
            pltpu.VMEM((z.node, z.rows, size), BF16),
            pltpu.VMEM((z.exp_dev, z.node * z.MP, size), BF16),
            pltpu.SemaphoreType.DMA((len(pieces),)),
            pltpu.SemaphoreType.DMA((z.exp_dev,)),
            pltpu.SemaphoreType.DMA((z.exp_dev,)),
        ],
        compiler_params=params(40),
        cost_estimate=pl.CostEstimate(
            flops=4 * z.exp_dev * z.node * z.MP * size * z.hidden,
            bytes_accessed=4 * z.exp_dev * size * z.hidden,
            transcendentals=0,
        ),
        name="up_chunk",
    )(*pieces, regroup, w_gate, w_up, *(() if first else sums))


def down_kernel(z, lo, size, order, hidden_ref, ungroup_ref, wd_ref, *refs):
    outs, (weight_ref, held_ref, sem) = refs[: len(order)], refs[len(order) :]

    def weights(e):
        return pltpu.make_async_copy(wd_ref.at[e, :, pl.ds(lo, size)], weight_ref.at[e], sem.at[e])

    for e in range(z.exp_dev):
        weights(e).start()

    def expert(e, carry):
        weights(e).wait()
        got = jnp.dot(hidden_ref[e], weight_ref[e], preferred_element_type=F32).astype(BF16)
        for m in range(z.node):
            held_ref[m, pl.ds(pl.multiple_of(e * z.MP, z.MP), z.MP), :] = got[m * z.MP : (m + 1) * z.MP]
        return carry

    lax.fori_loop(0, z.exp_dev, expert, 0)
    tile = tile_of(size)

    def step(i, carry):
        cols = pl.ds(pl.multiple_of(i * tile, tile), tile)
        for out, ms in zip(outs, order):
            for k, m in enumerate(ms):
                back = jnp.dot(ungroup_ref[...], held_ref[m, :, cols], preferred_element_type=F32).astype(BF16)
                for s in range(z.local):
                    out[k * z.local + s, :, cols] = back[s * z.RP : s * z.RP + z.R]
        return carry

    lax.fori_loop(0, size // tile, step, 0)


def down_chunk(z, c, hidden, ungroup, w_down, order):
    lo, size = z.down[c]
    shapes = [jax.ShapeDtypeStruct((len(ms) * z.local, z.R, size), BF16) for ms in order]
    return pl.pallas_call(
        functools.partial(down_kernel, z, lo, size, order),
        out_shape=shapes,
        in_specs=[in_vmem(), in_vmem(), in_hbm()],
        out_specs=[in_vmem()] * len(shapes),
        scratch_shapes=[
            pltpu.VMEM((z.exp_dev, z.hidden, size), BF16),
            pltpu.VMEM((z.node, z.grouped, size), BF16),
            pltpu.SemaphoreType.DMA((z.exp_dev,)),
        ],
        compiler_params=params(32),
        cost_estimate=pl.CostEstimate(
            flops=2 * z.exp_dev * z.node * z.MP * size * z.hidden,
            bytes_accessed=2 * z.exp_dev * size * z.hidden,
            transcendentals=0,
        ),
        name="down_chunk",
    )(hidden, ungroup, w_down)


def add_kernel(cuts, a_ref, b_ref, *outs):
    for out, (lo, hi, start) in zip(outs, cuts):
        out[...] = (a_ref[lo + start : hi + start].astype(F32) + b_ref[lo:hi].astype(F32)).astype(BF16)


def add_cut(a, b, cuts, start=0):
    total = sum(hi - lo for lo, hi in cuts) * a.shape[1] * a.shape[2]
    return pl.pallas_call(
        functools.partial(add_kernel, [(lo, hi, start) for lo, hi in cuts]),
        out_shape=[jax.ShapeDtypeStruct((hi - lo,) + a.shape[1:], BF16) for lo, hi in cuts],
        in_specs=[in_vmem()] * 2,
        out_specs=[in_vmem()] * len(cuts),
        compiler_params=params(32),
        cost_estimate=pl.CostEstimate(flops=total, bytes_accessed=6 * total, transcendentals=0),
        name="add_cut",
    )(a, b)


def combine_kernel(z, lo, size, blocks, weight_ref, *refs):
    pieces, (out_ref, rows_ref) = refs[: len(blocks)], refs[-2:]
    rows_ref[...] = jnp.zeros_like(rows_ref)
    for ref, (at, count) in zip(pieces, blocks):
        for i in range(count):
            rows_ref[at + i * z.RP : at + i * z.RP + z.R, :] = ref[i]
    weight = weight_ref[...].T
    extra = rows_ref.shape[0] - z.rows
    if extra:
        weight = jnp.concatenate([weight, weight[:, :extra]], axis=1)
    high = weight.astype(BF16)
    rest = weight - high.astype(F32)
    middle = rest.astype(BF16)
    low = (rest - middle.astype(F32)).astype(BF16)
    rows = rows_ref[...]
    total = jnp.dot(low, rows, preferred_element_type=F32)
    total = total + jnp.dot(middle, rows, preferred_element_type=F32)
    total = total + jnp.dot(high, rows, preferred_element_type=F32)
    out_ref[...] = total.astype(BF16)


def combine_chunk(z, c, weight, pieces, so_far):
    lo, size = z.down[c]
    blocks = [(at, count) for _, at, count in pieces]
    rows = max(at + count * z.RP for at, count in blocks)
    extra = [] if so_far is None else [so_far]
    return pl.pallas_call(
        functools.partial(combine_kernel, z, lo, size, blocks),
        grid=(1,),
        out_shape=jax.ShapeDtypeStruct((z.tok, z.width), BF16),
        in_specs=[pl.BlockSpec(weight.shape, lambda i: (0, 0))]
        + [pl.BlockSpec((n,) + p.shape[1:], lambda i: (0, 0, 0)) for p, _, n in pieces]
        + [in_hbm()] * len(extra),
        out_specs=pl.BlockSpec((z.tok, size), lambda i: (0, lo // size)),
        scratch_shapes=[pltpu.VMEM((rows, size), BF16)],
        input_output_aliases={1 + len(pieces): 0} if extra else {},
        compiler_params=params(32),
        name="combine_chunk",
    )(weight, *[p for p, _, _ in pieces], *extra)


def swap(a, mask, count):
    return lax.ppermute(a, "node", [(i, i ^ mask) for i in range(count)])


def shift(a, by, count):
    return lax.ppermute(a, "local", [(i, (i + by) % count) for i in range(count)])


def spread(a, masks, count):
    held = {0: a}
    for mask in reversed(masks):
        for m in list(held):
            held[m | mask] = swap(held[m], mask, count)
    return held


def per_device(tokens, expert_ids, gate_weights, w_gate, w_up, w_down):
    local_count, node_count = lax.axis_size("local"), lax.axis_size("node")
    z = Sizes(tokens, w_gate, local_count, node_count)
    plane = lax.axis_index("local").astype(jnp.int32).reshape(1)
    regroup = z.regroup()
    ungroup = jnp.asarray(regroup.T, BF16)
    regroup = jnp.asarray(regroup, BF16)
    weight, own, sent = gather_rows(z, plane, expert_ids, gate_weights, tokens)
    masks = []
    while 1 << len(masks) < node_count:
        masks.append(1 << len(masks))

    if z.relative:
        own_held = spread(own, masks, node_count)
    sums = None
    for c in range(len(z.up)):
        if z.relative:
            came = [shift(sent[c][s - 1], s, local_count) for s in range(1, local_count)]
            held = spread(jnp.concatenate(came, axis=0), masks, node_count)
            pieces = [a for m in range(node_count) for a in (own_held[m], held[m])]
        else:
            held = spread(lax.all_to_all(sent[c][0], "local", 0, 0, tiled=True), masks, node_count)
            pieces = [held[m] for m in range(node_count)]
        sums = up_chunk(z, c, pieces, regroup, w_gate, w_up, sums)
    hidden = sums[0]

    out = None
    count = local_count
    for c in range(len(z.down)):
        away = [m for m in range(node_count) if m & 1]
        kept = [m for m in range(node_count) if not m & 1]
        send, keep = down_chunk(z, c, hidden, ungroup, w_down, [away, kept])
        for mask in masks[:-1]:
            got = swap(send, mask, node_count)
            stay = [m for m in kept if not m & (mask << 1)]
            go = [m for m in kept if m & (mask << 1)]
            place = {m: i * count for i, m in enumerate(kept)}
            if mask << 1 == masks[-1] and z.relative:
                keep, send, send_own = add_cut(keep, got, [(0, count), (count + 1, 2 * count), (count, count + 1)])
            else:
                sums = add_cut(keep, got, [(place[m], place[m] + count) for m in stay + go])
                keep, send = sums if len(sums) == 2 else (
                    jnp.concatenate(sums[: len(stay)], axis=0),
                    jnp.concatenate(sums[len(stay) :], axis=0),
                )
            kept = stay
        got = swap(send, masks[-1], node_count)
        if z.relative:
            got_own = swap(send_own, masks[-1], node_count)
            parts = add_cut(keep, got, [(s, s + 1) for s in range(count - 1)], start=1)
            back = [shift(parts[s - 1], -s, count) for s in range(1, count)]
            pieces = [(keep, 0, 1)] + [(b, (s + 1) * z.RP, 1) for s, b in enumerate(back)] + [(got_own, z.rows, 1)]
        else:
            (summed,) = add_cut(keep, got, [(0, count)])
            pieces = [(lax.all_to_all(summed, "local", 0, 0, tiled=True), 0, count)]
        out = combine_chunk(z, c, weight, pieces, out)
    return out


def solution(mesh):
    return jax.shard_map(
        per_device,
        mesh=mesh,
        in_specs=(
            P(("parts", "node", "local"), None),
            P(("parts", "node", "local"), None),
            P(("parts", "node", "local"), None),
            P("local", None, "node"),
            P("local", None, "node"),
            P("local", "node", None),
        ),
        out_specs=P(("parts", "node", "local"), None),
        check_vma=False,
    )
```

```python
import functools

import jax
import jax.numpy as jnp
import numpy as np
from jax import lax
from jax.experimental import pallas as pl
from jax.experimental.pallas import tpu as pltpu
from jax.sharding import PartitionSpec as P

CAP = 5
UP_PARTS = (1, 1, 1, 1)
DOWN_PARTS = (1, 1, 1, 1)
WINDOW = 3
MIB = 1024 * 1024
F32, BF16 = jnp.float32, jnp.bfloat16


def pad16(n):
    return -(-n // 16) * 16


def params(mib):
    return pltpu.CompilerParams(vmem_limit_bytes=mib * MIB)


def in_vmem():
    return pl.BlockSpec(memory_space=pltpu.VMEM)


def in_hbm():
    return pl.BlockSpec(memory_space=pl.ANY)


def tie(a, *after):
    return lax.optimization_barrier((a,) + after)[0]


def cut(width, parts):
    unit = width // sum(parts)
    edges = [sum(parts[:i]) * unit for i in range(len(parts) + 1)]
    return list(zip(edges[:-1], [b - a for a, b in zip(edges[:-1], edges[1:])]))


def tile_of(width):
    for t in (512, 256, 128):
        if width % t == 0:
            return t
    return width


class Sizes:
    def __init__(self, tokens, w_gate, local_count, node_count):
        self.tok, self.width = tokens.shape
        self.exp_dev = w_gate.shape[0]
        self.hidden = w_gate.shape[2]
        self.local = local_count
        self.node = node_count
        self.R = self.exp_dev * CAP
        self.RP = pad16(self.R)
        self.MP = pad16(self.local * CAP)
        self.rows = self.local * self.RP
        self.grouped = self.exp_dev * self.MP
        self.relative = local_count <= 4 and node_count == 4
        self.up = cut(self.width, UP_PARTS)
        self.down = cut(self.width, DOWN_PARTS)

    def columns(self):
        table = np.full((self.rows, 4), -1, np.int32)
        for s in range(self.local):
            table[s * self.RP : (s + 1) * self.RP, 0] = s
            for q in range(self.R):
                table[s * self.RP + q, 1:3] = (q // CAP, q % CAP)
        return table

    def regroup(self):
        m = np.zeros((self.grouped, self.rows), np.float32)
        for s in range(self.local):
            for j in range(self.exp_dev):
                for c in range(CAP):
                    m[j * self.MP + s * CAP + c, s * self.RP + j * CAP + c] = 1
        return m


def gather_kernel(z, plan, plane_ref, table_ref, ids_ref, gates_ref, tokens_ref, weight_ref, *outs):
    block, expert, slot = (table_ref[:, i : i + 1] for i in range(3))
    plane = block
    if z.relative:
        plane = block + plane_ref[0]
        plane = jnp.where(plane >= z.local, plane - z.local, plane)
    name = jnp.where(slot >= 0, plane * z.exp_dev + expert, -1)
    ids, gates = ids_ref[...], gates_ref[...]
    top = ids.shape[0]
    hits = [ids[k : k + 1, :] == name for k in range(top)]
    named = hits[0].astype(F32)
    for k in range(1, top):
        named = named + hits[k].astype(F32)
    t0 = lax.broadcasted_iota(jnp.int32, (z.tok, z.tok), 0)
    t1 = lax.broadcasted_iota(jnp.int32, (z.tok, z.tok), 1)
    before = jnp.where(t0 < t1, 1.0, 0.0).astype(BF16)
    rank = jnp.dot(named.astype(BF16), before, preferred_element_type=F32)
    here = rank == slot.astype(F32)
    weight = jnp.zeros((z.rows, z.tok), F32)
    for k in range(top):
        weight = weight + jnp.where(hits[k] & here, gates[k : k + 1, :], 0.0)
    weight_ref[...] = weight
    pick = jnp.where(here, named, 0.0).astype(BF16)
    for lo, size, targets in plan:
        picked = jnp.dot(pick, tokens_ref[:, lo : lo + size], preferred_element_type=F32).astype(BF16)
        for s, (out, i, at) in enumerate(targets):
            outs[out][i, :, at : at + size] = picked[s * z.RP : s * z.RP + z.R]


def gather_rows(z, plane, ids, gates, tokens):
    shapes, plan = [], []
    if z.relative:
        shapes.append((1, z.R, z.width))
    for lo, size in z.up:
        if z.relative:
            n = len(shapes)
            shapes += [(1, z.R, size)] * (z.local - 1)
            targets = [(0, 0, lo)] + [(n + s, 0, 0) for s in range(z.local - 1)]
        else:
            targets = [(len(shapes), s, 0) for s in range(z.local)]
            shapes.append((z.local, z.R, size))
        plan.append((lo, size, targets))
    outs = pl.pallas_call(
        functools.partial(gather_kernel, z, plan),
        out_shape=[jax.ShapeDtypeStruct((z.rows, z.tok), F32)] + [jax.ShapeDtypeStruct(s, BF16) for s in shapes],
        in_specs=[pl.BlockSpec(memory_space=pltpu.SMEM)] + [in_vmem()] * 4,
        out_specs=[in_vmem()] * (1 + len(shapes)),
        compiler_params=params(32),
        name="gather_rows",
    )(plane, jnp.asarray(z.columns()), ids.T, gates.T, tokens)
    weight, outs = outs[0], list(outs[1:])
    own = outs.pop(0) if z.relative else None
    each = z.local - 1 if z.relative else 1
    return weight, own, [outs[i * each : (i + 1) * each] for i in range(len(z.up))]


def up_kernel(z, lo, size, places, first, last, *refs):
    pieces = refs[: len(places)]
    regroup_ref, wg_ref, wu_ref = refs[len(places) : len(places) + 3]
    refs = refs[len(places) + 3 :]
    if not first:
        gin_ref, uin_ref = refs[:2]
        refs = refs[2:]
    if last:
        hidden_ref = refs[0]
        refs = refs[1:]
    else:
        gout_ref, uout_ref = refs[:2]
        refs = refs[2:]
    piece_ref, gate_ref, up_ref, rows_ref, grouped_ref, psem, gsem, usem = refs

    moves, at = [], 0
    for i, (ref, where) in enumerate(zip(pieces, places)):
        src = ref if ref.shape[2] == size else ref.at[:, :, pl.ds(lo, size)]
        moves.append(pltpu.make_async_copy(src, piece_ref.at[pl.ds(at, len(where))], psem.at[i]))
        moves[-1].start()
        at += len(where)

    def weights(e):
        return (
            pltpu.make_async_copy(wg_ref.at[e, pl.ds(lo, size)], gate_ref.at[e], gsem.at[e]),
            pltpu.make_async_copy(wu_ref.at[e, pl.ds(lo, size)], up_ref.at[e], usem.at[e]),
        )

    for e in range(z.exp_dev):
        for move in weights(e):
            move.start()
    if z.RP > z.R:
        rows_ref[...] = jnp.zeros_like(rows_ref)
    at = 0
    for move, where in zip(moves, places):
        move.wait()
        for m, block in where:
            rows_ref[m, block * z.RP : block * z.RP + z.R, :] = piece_ref[at]
            at += 1
    tile = tile_of(size)

    def step(i, carry):
        cols = pl.ds(pl.multiple_of(i * tile, tile), tile)
        for m in range(z.node):
            got = jnp.dot(regroup_ref[...], rows_ref[m, :, cols], preferred_element_type=F32).astype(BF16)
            grouped_ref[:, m * z.MP : (m + 1) * z.MP, cols] = got.reshape(z.exp_dev, z.MP, tile)
        return carry

    lax.fori_loop(0, size // tile, step, 0)

    def expert(e, carry):
        for move in weights(e):
            move.wait()
        rows = grouped_ref[e]
        gate = jnp.dot(rows, gate_ref[e], preferred_element_type=F32)
        up = jnp.dot(rows, up_ref[e], preferred_element_type=F32)
        if not first:
            gate = gate + gin_ref[e]
            up = up + uin_ref[e]
        if last:
            hidden_ref[e] = (gate / (1.0 + jnp.exp(-gate)) * up).astype(BF16)
        else:
            gout_ref[e] = gate
            uout_ref[e] = up
        return carry

    lax.fori_loop(0, z.exp_dev, expert, 0)


def up_chunk(z, c, pieces, regroup, w_gate, w_up, sums):
    lo, size = z.up[c]
    first, last = sums is None, c == len(z.up) - 1
    pieces, places = zip(*pieces)
    acc = jax.ShapeDtypeStruct((z.exp_dev, z.node * z.MP, z.hidden), F32)
    out_shape = [jax.ShapeDtypeStruct(acc.shape, BF16)] if last else [acc, acc]
    return pl.pallas_call(
        functools.partial(up_kernel, z, lo, size, places, first, last),
        out_shape=out_shape,
        in_specs=[in_hbm()] * len(pieces) + [in_vmem(), in_hbm(), in_hbm()] + ([] if first else [in_vmem()] * 2),
        out_specs=[in_vmem()] * len(out_shape),
        scratch_shapes=[
            pltpu.VMEM((z.node * z.local, z.R, size), BF16),
            pltpu.VMEM((z.exp_dev, size, z.hidden), BF16),
            pltpu.VMEM((z.exp_dev, size, z.hidden), BF16),
            pltpu.VMEM((z.node, z.rows, size), BF16),
            pltpu.VMEM((z.exp_dev, z.node * z.MP, size), BF16),
            pltpu.SemaphoreType.DMA((len(pieces),)),
            pltpu.SemaphoreType.DMA((z.exp_dev,)),
            pltpu.SemaphoreType.DMA((z.exp_dev,)),
        ],
        compiler_params=params(40),
        cost_estimate=pl.CostEstimate(
            flops=4 * z.exp_dev * z.node * z.MP * size * z.hidden,
            bytes_accessed=4 * z.exp_dev * size * z.hidden,
            transcendentals=0,
        ),
        name="up_chunk",
    )(*pieces, regroup, w_gate, w_up, *(() if first else sums))


def down_kernel(z, lo, size, order, hidden_ref, ungroup_ref, wd_ref, *refs):
    outs, (weight_ref, held_ref, sem) = refs[: len(order)], refs[len(order) :]

    def weights(e):
        return pltpu.make_async_copy(wd_ref.at[e, :, pl.ds(lo, size)], weight_ref.at[e], sem.at[e])

    for e in range(z.exp_dev):
        weights(e).start()

    def expert(e, carry):
        weights(e).wait()
        got = jnp.dot(hidden_ref[e], weight_ref[e], preferred_element_type=F32).astype(BF16)
        for m in range(z.node):
            held_ref[m, pl.ds(pl.multiple_of(e * z.MP, z.MP), z.MP), :] = got[m * z.MP : (m + 1) * z.MP]
        return carry

    lax.fori_loop(0, z.exp_dev, expert, 0)
    tile = tile_of(size)

    def step(i, carry):
        cols = pl.ds(pl.multiple_of(i * tile, tile), tile)
        for out, ms in zip(outs, order):
            for k, m in enumerate(ms):
                back = jnp.dot(ungroup_ref[...], held_ref[m, :, cols], preferred_element_type=F32).astype(BF16)
                for s in range(z.local):
                    out[k * z.local + s, :, cols] = back[s * z.RP : s * z.RP + z.R]
        return carry

    lax.fori_loop(0, size // tile, step, 0)


def down_chunk(z, c, hidden, ungroup, w_down, order):
    lo, size = z.down[c]
    shapes = [jax.ShapeDtypeStruct((len(ms) * z.local, z.R, size), BF16) for ms in order]
    return pl.pallas_call(
        functools.partial(down_kernel, z, lo, size, order),
        out_shape=shapes,
        in_specs=[in_vmem(), in_vmem(), in_hbm()],
        out_specs=[in_vmem()] * len(shapes),
        scratch_shapes=[
            pltpu.VMEM((z.exp_dev, z.hidden, size), BF16),
            pltpu.VMEM((z.node, z.grouped, size), BF16),
            pltpu.SemaphoreType.DMA((z.exp_dev,)),
        ],
        compiler_params=params(32),
        cost_estimate=pl.CostEstimate(
            flops=2 * z.exp_dev * z.node * z.MP * size * z.hidden,
            bytes_accessed=2 * z.exp_dev * size * z.hidden,
            transcendentals=0,
        ),
        name="down_chunk",
    )(hidden, ungroup, w_down)


def add_kernel(cuts, a_ref, b_ref, *outs):
    for out, (lo, hi, start) in zip(outs, cuts):
        out[...] = (a_ref[lo + start : hi + start].astype(F32) + b_ref[lo:hi].astype(F32)).astype(BF16)


def add_cut(a, b, cuts, start=0):
    total = sum(hi - lo for lo, hi in cuts) * a.shape[1] * a.shape[2]
    return pl.pallas_call(
        functools.partial(add_kernel, [(lo, hi, start) for lo, hi in cuts]),
        out_shape=[jax.ShapeDtypeStruct((hi - lo,) + a.shape[1:], BF16) for lo, hi in cuts],
        in_specs=[in_vmem()] * 2,
        out_specs=[in_vmem()] * len(cuts),
        compiler_params=params(32),
        cost_estimate=pl.CostEstimate(flops=total, bytes_accessed=6 * total, transcendentals=0),
        name="add_cut",
    )(a, b)


def combine_kernel(z, lo, size, blocks, weight_ref, *refs):
    pieces, (out_ref, rows_ref) = refs[: len(blocks)], refs[-2:]
    rows_ref[...] = jnp.zeros_like(rows_ref)
    for ref, (at, count) in zip(pieces, blocks):
        for i in range(count):
            rows_ref[at + i * z.RP : at + i * z.RP + z.R, :] = ref[i]
    weight = weight_ref[...].T
    extra = rows_ref.shape[0] - z.rows
    if extra:
        weight = jnp.concatenate([weight, weight[:, :extra]], axis=1)
    high = weight.astype(BF16)
    rest = weight - high.astype(F32)
    middle = rest.astype(BF16)
    low = (rest - middle.astype(F32)).astype(BF16)
    rows = rows_ref[...]
    total = jnp.dot(low, rows, preferred_element_type=F32)
    total = total + jnp.dot(middle, rows, preferred_element_type=F32)
    total = total + jnp.dot(high, rows, preferred_element_type=F32)
    out_ref[...] = total.astype(BF16)


def combine_chunk(z, c, weight, pieces, so_far):
    lo, size = z.down[c]
    blocks = [(at, count) for _, at, count in pieces]
    rows = max(at + count * z.RP for at, count in blocks)
    extra = [] if so_far is None else [so_far]
    return pl.pallas_call(
        functools.partial(combine_kernel, z, lo, size, blocks),
        grid=(1,),
        out_shape=jax.ShapeDtypeStruct((z.tok, z.width), BF16),
        in_specs=[pl.BlockSpec(weight.shape, lambda i: (0, 0))]
        + [
            pl.BlockSpec((n, z.R, size), lambda i, at=lo // size if p.shape[2] != size else 0: (0, 0, at))
            for p, _, n in pieces
        ]
        + [in_hbm()] * len(extra),
        out_specs=pl.BlockSpec((z.tok, size), lambda i: (0, lo // size)),
        scratch_shapes=[pltpu.VMEM((rows, size), BF16)],
        input_output_aliases={1 + len(pieces): 0} if extra else {},
        compiler_params=params(32),
        name="combine_chunk",
    )(weight, *[p for p, _, _ in pieces], *extra)


def swap(a, mask, count):
    return lax.ppermute(a, "node", [(i, i ^ mask) for i in range(count)])


def shift(a, by, count):
    return lax.ppermute(a, "local", [(i, (i + by) % count) for i in range(count)])


def concat(*arrays):
    return jnp.concatenate(arrays, axis=0)


def per_device(tokens, expert_ids, gate_weights, w_gate, w_up, w_down):
    local_count, node_count = lax.axis_size("local"), lax.axis_size("node")
    z = Sizes(tokens, w_gate, local_count, node_count)
    plane = lax.axis_index("local").astype(jnp.int32).reshape(1)
    regroup = z.regroup()
    ungroup = jnp.asarray(regroup.T, BF16)
    regroup = jnp.asarray(regroup, BF16)
    weight, own, sent = gather_rows(z, plane, expert_ids, gate_weights, tokens)
    route = by_distance if z.relative else by_plane
    return route(z, weight, own, sent, w_gate, w_up, w_down, regroup, ungroup)


def by_distance(z, weight, own, sent, w_gate, w_up, w_down, regroup, ungroup):
    count = z.local
    near, far = swap(own, 1, 4), swap(own, 2, 4)
    both = swap(far, 1, 4)
    hold = [near, far, both]
    order = sorted(range(1, count), key=lambda s: -min(s, count - s))
    came, done = {}, []
    for c in range(len(z.up)):
        for s in order:
            after = done[-WINDOW:][:1] if len(done) >= WINDOW else []
            if c > 0 and s == order[0] and hold:
                after = after + [hold.pop(0)]
            a = sent[c][s - 1]
            came[c, s] = shift(tie(a, *after) if after else a, s, count)
            done.append(came[c, s])
    sums, history = None, []
    blocks = range(1, count)
    for c in range(len(z.up)):
        stack = concat(*[came[c, s] for s in blocks])
        pair = concat(stack, swap(stack, 2, 4))
        if len(history) >= 2:
            pair = tie(pair, *history[-2])
        pieces = [
            (own, [(0, 0)]),
            (near, [(1, 0)]),
            (far, [(2, 0)]),
            (both, [(3, 0)]),
            (pair, [(m, s) for m in (0, 2) for s in blocks]),
            (swap(pair, 1, 4), [(m, s) for m in (1, 3) for s in blocks]),
        ]
        sums = up_chunk(z, c, pieces, regroup, w_gate, w_up, sums)
        history.append(sums)
    hidden = sums[0]

    keep, got, send_own = [], [], []
    for c in range(len(z.down)):
        send, kept = down_chunk(z, c, hidden, ungroup, w_down, [[1, 3], [0, 2]])
        k, away, away_own = add_cut(
            kept, swap(send, 1, 4), [(0, count), (count + 1, 2 * count), (count, count + 1)]
        )
        keep.append(k)
        got.append(swap(away, 2, 4))
        send_own.append(away_own)
        hidden = tie(hidden, away)
    got_own = swap(tie(jnp.concatenate(send_own, axis=2), got[-1]), 2, 4)
    done, back = [], {}
    for c in range(len(z.down)):
        parts = add_cut(keep[c], got[c], [(s, s + 1) for s in range(count - 1)], start=1)
        for s in order:
            a = parts[s - 1]
            if len(done) >= WINDOW:
                a = tie(a, done[-WINDOW])
            back[c, s] = shift(a, -s, count)
            done.append(back[c, s])
    out = None
    for c in range(len(z.down)):
        pieces = [(keep[c], 0, 1)] + [(back[c, s], s * z.RP, 1) for s in blocks] + [(got_own, z.rows, 1)]
        out = combine_chunk(z, c, weight, pieces, out)
    return out


def spread(a, masks, count):
    held = {0: a}
    for mask in reversed(masks):
        for m in list(held):
            held[m | mask] = swap(held[m], mask, count)
    return held


def by_plane(z, weight, own, sent, w_gate, w_up, w_down, regroup, ungroup):
    count, masks = z.local, []
    while 1 << len(masks) < z.node:
        masks.append(1 << len(masks))
    sums = None
    for c in range(len(z.up)):
        held = spread(lax.all_to_all(sent[c][0], "local", 0, 0, tiled=True), masks, z.node)
        pieces = [(held[m], [(m, s) for s in range(count)]) for m in range(z.node)]
        sums = up_chunk(z, c, pieces, regroup, w_gate, w_up, sums)
    hidden, out = sums[0], None
    for c in range(len(z.down)):
        rows = dict(enumerate(down_chunk(z, c, hidden, ungroup, w_down, [[m] for m in range(z.node)])))
        for mask in masks:
            for m in [m for m in rows if not m & mask]:
                (rows[m],) = add_cut(rows[m], swap(rows.pop(m | mask), mask, z.node), [(0, count)])
        back = lax.all_to_all(rows[0], "local", 0, 0, tiled=True)
        out = combine_chunk(z, c, weight, [(back, 0, count)], out)
    return out


def solution(mesh):
    return jax.shard_map(
        per_device,
        mesh=mesh,
        in_specs=(
            P(("parts", "node", "local"), None),
            P(("parts", "node", "local"), None),
            P(("parts", "node", "local"), None),
            P("local", None, "node"),
            P("local", None, "node"),
            P("local", "node", None),
        ),
        out_specs=P(("parts", "node", "local"), None),
        check_vma=False,
    )
```

```python
import functools
import math

import jax
import jax.numpy as jnp
import numpy as np
from jax import lax
from jax.experimental import pallas as pl
from jax.experimental.pallas import tpu as pltpu
from jax.sharding import PartitionSpec as P

CAP = 5
GROUPS = 4
WINDOW = 3
MIB = 1024 * 1024
F32, BF16 = jnp.float32, jnp.bfloat16


def pad16(n):
    return -(-n // 16) * 16


def params(mib):
    return pltpu.CompilerParams(vmem_limit_bytes=mib * MIB)


def in_vmem():
    return pl.BlockSpec(memory_space=pltpu.VMEM)


def in_hbm():
    return pl.BlockSpec(memory_space=pl.ANY)


def tie(a, *after):
    return lax.optimization_barrier((a,) + after)[0] if after else a


def tile_of(width):
    for t in (512, 256, 128):
        if width % t == 0:
            return t
    return width


class Sizes:
    def __init__(self, tokens, w_gate, local_count, node_count):
        self.tok, self.width = tokens.shape
        self.exp_dev = w_gate.shape[0]
        self.hidden = w_gate.shape[2]
        self.local = local_count
        self.node = node_count
        self.groups = math.gcd(self.exp_dev, GROUPS)
        self.each = self.exp_dev // self.groups
        self.folds = math.gcd(max(1, 8 // self.each), self.width // 128)
        self.dc = self.width // self.folds
        self.V = self.folds * self.each
        self.R = self.V * CAP
        self.RP = pad16(self.R)
        self.MP = pad16(self.local * CAP)
        self.rows = self.local * self.RP
        self.grouped = self.V * self.MP
        self.relative = local_count <= 4 and node_count == 4

    def regroup(self):
        m = np.zeros((self.grouped, self.rows), np.float32)
        for s in range(self.local):
            for j in range(self.V):
                for c in range(CAP):
                    m[j * self.MP + s * CAP + c, s * self.RP + j * CAP + c] = 1
        return m


def steps(a, width, count):
    total = jnp.zeros_like(a)
    for i in range(1, count):
        total = total + (a >= i * width).astype(jnp.int32)
    return total


def slots(z, group, plane_ref, ids):
    row = lax.broadcasted_iota(jnp.int32, (z.rows, 1), 0)
    block = steps(row, z.RP, z.local)
    place = row - block * z.RP
    both = steps(place, CAP, z.V + 1)
    slot = place - both * CAP
    fold = steps(both, z.each, z.folds)
    expert = both - fold * z.each
    plane = block
    if z.relative:
        plane = block + plane_ref[0]
        plane = jnp.where(plane >= z.local, plane - z.local, plane)
    name = jnp.where(place < z.R, plane * z.exp_dev + group * z.each + expert, -1)
    hits = [ids[k : k + 1, :] == name for k in range(ids.shape[0])]
    named = hits[0].astype(F32)
    for hit in hits[1:]:
        named = named + hit.astype(F32)
    t0 = lax.broadcasted_iota(jnp.int32, (z.tok, z.tok), 0)
    t1 = lax.broadcasted_iota(jnp.int32, (z.tok, z.tok), 1)
    before = jnp.where(t0 < t1, 1.0, 0.0).astype(BF16)
    rank = jnp.dot(named.astype(BF16), before, preferred_element_type=F32)
    here = rank == slot.astype(F32)
    return named, here, hits, fold


def gather_kernel(z, plane_ref, ids_ref, tokens_ref, *refs):
    outs, (names_ref, stack_ref, sem) = refs[:-3], refs[-3:]
    moves = [pltpu.make_async_copy(ids_ref, names_ref, sem.at[0])]
    for q in range(z.folds):
        src = tokens_ref.at[:, pl.ds(q * z.dc, z.dc)]
        moves.append(pltpu.make_async_copy(src, stack_ref.at[pl.ds(q * z.tok, z.tok)], sem.at[1 + q]))
    for move in moves:
        move.start()
    moves[0].wait()
    picks = []
    for g in range(z.groups):
        named, here, _, fold = slots(z, g, plane_ref, names_ref[...])
        pick = jnp.where(here, named, 0.0)
        picks.append(jnp.concatenate([jnp.where(fold == q, pick, 0.0) for q in range(z.folds)], axis=1).astype(BF16))
    for move in moves[1:]:
        move.wait()
    tile = tile_of(z.dc)

    def step(i, carry):
        cols = pl.ds(pl.multiple_of(i * tile, tile), tile)
        for g in range(z.groups):
            got = jnp.dot(picks[g], stack_ref[:, cols], preferred_element_type=F32).astype(BF16)
            for s in range(z.local):
                value = got[s * z.RP : s * z.RP + z.R]
                if not z.relative:
                    outs[g][s, :, cols] = value
                elif s == 0:
                    outs[0][g, :, cols] = value
                else:
                    outs[1 + g * (z.local - 1) + s - 1][0, :, cols] = value
        return carry

    lax.fori_loop(0, z.dc // tile, step, 0)


def gather_rows(z, plane, ids, tokens):
    if z.relative:
        shapes = [(z.groups, z.R, z.dc)] + [(1, z.R, z.dc)] * (z.groups * (z.local - 1))
    else:
        shapes = [(z.local, z.R, z.dc)] * z.groups
    outs = pl.pallas_call(
        functools.partial(gather_kernel, z),
        out_shape=[jax.ShapeDtypeStruct(s, BF16) for s in shapes],
        in_specs=[pl.BlockSpec(memory_space=pltpu.SMEM)] + [in_hbm()] * 2,
        out_specs=[in_vmem()] * len(shapes),
        scratch_shapes=[
            pltpu.VMEM((ids.shape[1], z.tok), jnp.int32),
            pltpu.VMEM((z.folds * z.tok, z.dc), BF16),
            pltpu.SemaphoreType.DMA((1 + z.folds,)),
        ],
        compiler_params=params(40),
        name="gather_rows",
    )(plane, ids.T, tokens)
    outs = list(outs)
    own = outs.pop(0) if z.relative else None
    each = z.local - 1 if z.relative else 1
    return own, [outs[i * each : (i + 1) * each] for i in range(z.groups)]


def weight_kernel(z, plane_ref, ids_ref, gates_ref, out_ref):
    gates = gates_ref[...]
    size = z.folds * z.tok
    for g in range(z.groups):
        _, here, hits, fold = slots(z, g, plane_ref, ids_ref[...])
        weight = jnp.zeros((z.rows, z.tok), F32)
        for k, hit in enumerate(hits):
            weight = weight + jnp.where(hit & here, gates[k : k + 1, :], 0.0)
        for q in range(z.folds):
            mine = jnp.where(fold == q, weight, 0.0).T
            high = mine.astype(BF16)
            out_ref[g, q * z.tok : (q + 1) * z.tok, :] = high
            out_ref[g, size + q * z.tok : size + (q + 1) * z.tok, :] = (mine - high.astype(F32)).astype(BF16)


def combine_weights(z, plane, ids, gates):
    return pl.pallas_call(
        functools.partial(weight_kernel, z),
        out_shape=jax.ShapeDtypeStruct((z.groups, 2 * z.folds * z.tok, z.rows), BF16),
        in_specs=[pl.BlockSpec(memory_space=pltpu.SMEM)] + [in_vmem()] * 2,
        out_specs=in_vmem(),
        compiler_params=params(40),
        name="combine_weights",
    )(plane, ids.T, gates.T)


def expert_kernel(z, group, places, order, *refs):
    pieces = refs[: len(places)]
    regroup_ref, ungroup_ref, wg_ref, wu_ref, wd_ref = refs[len(places) : len(places) + 5]
    outs = refs[len(places) + 5 : len(places) + 5 + len(order)]
    piece_ref, gate_ref, up_ref, down_ref, rows_ref, grouped_ref, hidden_ref, psem, wsem = refs[
        len(places) + 5 + len(order) :
    ]
    moves, at = [], 0
    for i, (ref, where) in enumerate(zip(pieces, places)):
        moves.append(pltpu.make_async_copy(ref, piece_ref.at[pl.ds(at, len(where))], psem.at[i]))
        moves[-1].start()
        at += len(where)
    loads = []
    for j in range(z.each):
        e = group * z.each + j
        for i, (src, dst) in enumerate(((wg_ref, gate_ref), (wu_ref, up_ref), (wd_ref, down_ref))):
            loads.append(pltpu.make_async_copy(src.at[e], dst.at[j], wsem.at[3 * j + i]))
    for i in [k for k in range(3 * z.each) if k % 3 < 2] + [k for k in range(3 * z.each) if k % 3 == 2]:
        loads[i].start()

    if z.RP > z.R:
        rows_ref[...] = jnp.zeros_like(rows_ref)
    at = 0
    for move, where in zip(moves, places):
        move.wait()
        for m, block in where:
            rows_ref[m, block * z.RP : block * z.RP + z.R, :] = piece_ref[at]
            at += 1
    tile = tile_of(z.dc)

    def step(i, carry):
        cols = pl.ds(pl.multiple_of(i * tile, tile), tile)
        for m in range(z.node):
            got = jnp.dot(regroup_ref[...], rows_ref[m, :, cols], preferred_element_type=F32).astype(BF16)
            got = got.reshape(z.V, z.MP, tile)
            for q in range(z.folds):
                there = pl.ds(pl.multiple_of(q * z.dc + i * tile, tile), tile)
                grouped_ref[:, m * z.MP : (m + 1) * z.MP, there] = got[q * z.each : (q + 1) * z.each]
        return carry

    lax.fori_loop(0, z.dc // tile, step, 0)

    for j in range(z.each):
        loads[3 * j].wait()
        gate = jnp.dot(grouped_ref[j], gate_ref[j], preferred_element_type=F32)
        loads[3 * j + 1].wait()
        up = jnp.dot(grouped_ref[j], up_ref[j], preferred_element_type=F32)
        hidden_ref[j] = (gate / (1.0 + jnp.exp(-gate)) * up).astype(BF16)

    for j in range(z.each):
        loads[3 * j + 2].wait()
        for q in range(z.folds):
            there = slice(q * z.dc, (q + 1) * z.dc)
            got = jnp.dot(hidden_ref[j], down_ref[j, :, there], preferred_element_type=F32)
            grouped_ref[j, :, there] = got.astype(BF16)

    def back(i, carry):
        cols = pl.ds(pl.multiple_of(i * tile, tile), tile)
        for out, ms in zip(outs, order):
            for k, m in enumerate(ms):
                held = []
                for q in range(z.folds):
                    there = pl.ds(pl.multiple_of(q * z.dc + i * tile, tile), tile)
                    held.append(grouped_ref[:, m * z.MP : (m + 1) * z.MP, there].reshape(z.each * z.MP, tile))
                got = jnp.dot(ungroup_ref[...], concat(*held), preferred_element_type=F32).astype(BF16)
                for s in range(z.local):
                    out[k * z.local + s, :, cols] = got[s * z.RP : s * z.RP + z.R]
        return carry

    lax.fori_loop(0, z.dc // tile, back, 0)


def expert_group(z, group, pieces, regroup, ungroup, w_gate, w_up, w_down, order):
    pieces, places = zip(*pieces)
    shapes = [jax.ShapeDtypeStruct((len(ms) * z.local, z.R, z.dc), BF16) for ms in order]
    scratch = [
        ((z.node * z.local, z.R, z.dc), BF16),
        ((z.each, z.width, z.hidden), BF16),
        ((z.each, z.width, z.hidden), BF16),
        ((z.each, z.hidden, z.width), BF16),
        ((z.node, z.rows, z.dc), BF16),
        ((z.each, z.node * z.MP, z.width), BF16),
        ((z.each, z.node * z.MP, z.hidden), BF16),
    ]
    return pl.pallas_call(
        functools.partial(expert_kernel, z, group, places, order),
        out_shape=shapes,
        in_specs=[in_hbm()] * len(pieces) + [in_vmem()] * 2 + [in_hbm()] * 3,
        out_specs=[in_vmem()] * len(shapes),
        scratch_shapes=[pltpu.VMEM(s, t) for s, t in scratch]
        + [pltpu.SemaphoreType.DMA((len(pieces),)), pltpu.SemaphoreType.DMA((3 * z.each,))],
        compiler_params=params(48 if z.relative else 60),
        cost_estimate=pl.CostEstimate(
            flops=6 * z.each * z.node * z.MP * z.width * z.hidden,
            bytes_accessed=6 * z.each * z.width * z.hidden,
            transcendentals=0,
        ),
        name="expert_group",
    )(*pieces, regroup, ungroup, w_gate, w_up, w_down)


def add_kernel(cuts, a_ref, b_ref, *outs):
    for out, (lo, hi) in zip(outs, cuts):
        out[...] = (a_ref[lo:hi].astype(F32) + b_ref[lo:hi].astype(F32)).astype(BF16)


def add_cut(a, b, cuts):
    return pl.pallas_call(
        functools.partial(add_kernel, cuts),
        out_shape=[jax.ShapeDtypeStruct((hi - lo,) + a.shape[1:], BF16) for lo, hi in cuts],
        in_specs=[in_vmem()] * 2,
        out_specs=[in_vmem()] * len(cuts),
        compiler_params=params(32),
        cost_estimate=pl.CostEstimate(flops=a.size, bytes_accessed=6 * a.size, transcendentals=0),
        name="add_cut",
    )(a, b)


def combine_kernel(z, group, counts, last, weight_ref, *refs):
    pieces = refs[: len(counts)]
    refs = refs[len(counts) :]
    if group > 0:
        before_ref = refs[0]
        refs = refs[1:]
    out_ref, rows_ref = refs
    if z.RP > z.R:
        rows_ref[...] = jnp.zeros_like(rows_ref)
    at = 0
    for ref, count in zip(pieces, counts):
        for i in range(count):
            rows_ref[at * z.RP : at * z.RP + z.R, :] = ref[i]
            at += 1
    size = z.folds * z.tok
    tile = tile_of(z.dc)
    for i in range(z.dc // tile):
        cols = slice(i * tile, (i + 1) * tile)
        terms = jnp.dot(weight_ref[group], rows_ref[:, cols], preferred_element_type=F32)
        total = terms[:size] + terms[size:]
        if group > 0:
            total = total + before_ref[:, cols]
        if last:
            for q in range(z.folds):
                there = slice(q * z.dc + i * tile, q * z.dc + (i + 1) * tile)
                out_ref[:, there] = total[q * z.tok : (q + 1) * z.tok].astype(BF16)
        else:
            out_ref[:, cols] = total


def combine_group(z, group, weight, pieces, before):
    last = group == z.groups - 1
    shape = jax.ShapeDtypeStruct((z.tok, z.width), BF16) if last else jax.ShapeDtypeStruct((z.folds * z.tok, z.dc), F32)
    extra = [] if group == 0 else [before]
    return pl.pallas_call(
        functools.partial(combine_kernel, z, group, [p.shape[0] for p in pieces], last),
        out_shape=shape,
        in_specs=[in_vmem()] * (1 + len(pieces) + len(extra)),
        out_specs=in_vmem(),
        scratch_shapes=[pltpu.VMEM((z.rows, z.dc), BF16)],
        compiler_params=params(32),
        name="combine_group",
    )(weight, *pieces, *extra)


def swap(a, mask, count):
    return lax.ppermute(a, "node", [(i, i ^ mask) for i in range(count)])


def shift(a, by, count):
    return lax.ppermute(a, "local", [(i, (i + by) % count) for i in range(count)])


def concat(*arrays):
    return jnp.concatenate(arrays, axis=0)


def per_device(tokens, expert_ids, gate_weights, w_gate, w_up, w_down):
    local_count, node_count = lax.axis_size("local"), lax.axis_size("node")
    z = Sizes(tokens, w_gate, local_count, node_count)
    plane = lax.axis_index("local").astype(jnp.int32).reshape(1)
    regroup = z.regroup()
    matrices = jnp.asarray(regroup, BF16), jnp.asarray(regroup.T, BF16)
    own, sent = gather_rows(z, plane, expert_ids, tokens)
    weight = combine_weights(z, plane, expert_ids, gate_weights)
    route = by_distance if z.relative else by_plane
    return route(z, weight, own, sent, matrices, (w_gate, w_up, w_down))


def by_distance(z, weight, own, sent, matrices, weights):
    count, blocks = z.local, range(1, z.local)
    order = sorted(blocks, key=lambda s: -min(s, count - s))
    done, result = [], None

    def recent():
        return done[-WINDOW - 2 : len(done) - WINDOW + 1] if len(done) >= WINDOW else []

    far = swap(own, 2, 4)
    came = {}
    for g in range(z.groups):
        for s in order:
            came[g, s] = shift(tie(sent[g][s - 1], *recent()), s, count)
            done.append(came[g, s])
    stacks = [concat(*[came[g, s] for s in blocks]) for g in range(z.groups)]
    across = [swap(stack, 2, 4) for stack in stacks]
    pairs, beside = [], []

    def pair_up(*after):
        g = len(pairs)
        if g < z.groups:
            next_ones = [came[g + 1, s] for s in blocks] if g + 1 < z.groups else []
            a = tie(across[g], *next_ones, *after)
            pairs.append(concat(own[g : g + 1], stacks[g], far[g : g + 1], a))
            beside.append(swap(pairs[g], 1, 4))

    pair_up()
    pair_up()
    returned, away, summed, parts, back = [], [], [], [], []
    for g in range(z.groups):
        before = stacks[g + 2 : g + 3] + across[g + 1 : g + 2]
        before += away[g - 2 : g - 1] if g >= 2 else []
        before += parts[g - 3] if g >= 3 else []
        pieces = [(tie(pairs[g], *before), [(m, s) for m in (0, 2) for s in range(count)])]
        pieces.append((beside[g], [(m, s) for m in (1, 3) for s in range(count)]))
        send, kept = expert_group(z, g, pieces, *matrices, *weights, [[1, 3], [0, 2]])
        pair_up(send)
        beside_it = [came[g + 3, s] for s in blocks] if g + 3 < z.groups else []
        beside_it += across[g + 2 : g + 3] + beside[g + 1 : g + 2]
        beside_it += returned[g - 1 : g] if g >= 1 else []
        beside_it += summed[g - 2 : g - 1] if g >= 2 else []
        beside_it += list(back[g - 3].values()) if g >= 3 else []
        returned.append(swap(tie(send, *beside_it), 1, 4))
        keep, a = add_cut(kept, returned[g], [(0, count), (count, 2 * count)])
        away.append(a)
        summed.append(swap(a, 2, 4))
        parts.append(add_cut(keep, summed[g], [(s, s + 1) for s in range(count)]))
        back.append({})
        for s in order:
            back[g][s] = shift(tie(parts[g][s], *recent()), -s, count)
            done.append(back[g][s])
    for g in range(z.groups):
        result = combine_group(z, g, weight, [parts[g][0]] + [back[g][s] for s in blocks], result)
    return result


def spread(a, masks, count):
    held = {0: a}
    for mask in reversed(masks):
        for m in list(held):
            held[m | mask] = swap(held[m], mask, count)
    return held


def by_plane(z, weight, own, sent, matrices, weights):
    count, masks, result = z.local, [], None
    while 1 << len(masks) < z.node:
        masks.append(1 << len(masks))
    for g in range(z.groups):
        held = spread(lax.all_to_all(sent[g][0], "local", 0, 0, tiled=True), masks, z.node)
        pieces = [(held[m], [(m, s) for s in range(count)]) for m in range(z.node)]
        rows = expert_group(z, g, pieces, *matrices, *weights, [[m] for m in range(z.node)])
        rows = dict(enumerate(rows))
        for mask in masks:
            for m in [m for m in rows if not m & mask]:
                (rows[m],) = add_cut(rows[m], swap(rows.pop(m | mask), mask, z.node), [(0, count)])
        back = lax.all_to_all(rows[0], "local", 0, 0, tiled=True)
        result = combine_group(z, g, weight, [back], result)
    return result


def solution(mesh):
    return jax.shard_map(
        per_device,
        mesh=mesh,
        in_specs=(
            P(("parts", "node", "local"), None),
            P(("parts", "node", "local"), None),
            P(("parts", "node", "local"), None),
            P("local", None, "node"),
            P("local", None, "node"),
            P("local", "node", None),
        ),
        out_specs=P(("parts", "node", "local"), None),
        check_vma=False,
    )
```

```python
import functools
import math

import jax
import jax.numpy as jnp
import numpy as np
from jax import lax
from jax.experimental import pallas as pl
from jax.experimental.pallas import tpu as pltpu
from jax.sharding import PartitionSpec as P

CAP = 5
GROUPS = 4
WINDOW = 3
AHEAD = 3
LAG = 2
MIB = 1024 * 1024
F32, BF16 = jnp.float32, jnp.bfloat16


def pad16(n):
    return -(-n // 16) * 16


def params(mib):
    return pltpu.CompilerParams(vmem_limit_bytes=mib * MIB)


def in_vmem():
    return pl.BlockSpec(memory_space=pltpu.VMEM)


def in_hbm():
    return pl.BlockSpec(memory_space=pl.ANY)


def tie(a, *after):
    return lax.optimization_barrier((a,) + after)[0] if after else a


def tile_of(width):
    for t in (512, 256, 128):
        if width % t == 0:
            return t
    return width


class Sizes:
    def __init__(self, tokens, w_gate, local_count, node_count):
        self.tok, self.width = tokens.shape
        self.exp_dev = w_gate.shape[0]
        self.hidden = w_gate.shape[2]
        self.local = local_count
        self.node = node_count
        self.groups = math.gcd(self.exp_dev, GROUPS)
        self.each = self.exp_dev // self.groups
        self.folds = math.gcd(max(1, 8 // self.each), self.width // 128)
        self.dc = self.width // self.folds
        self.V = self.folds * self.each
        self.R = self.V * CAP
        self.RP = pad16(self.R)
        self.MP = pad16(self.local * CAP)
        self.rows = self.local * self.RP
        self.grouped = self.V * self.MP
        self.relative = local_count <= 4 and node_count == 4

    def regroup(self):
        m = np.zeros((self.grouped, self.rows), np.float32)
        for s in range(self.local):
            for j in range(self.V):
                for c in range(CAP):
                    m[j * self.MP + s * CAP + c, s * self.RP + j * CAP + c] = 1
        return m


def steps(a, width, count):
    total = jnp.zeros_like(a)
    for i in range(1, count):
        total = total + (a >= i * width).astype(jnp.int32)
    return total


def slots(z, group, plane_ref, ids):
    row = lax.broadcasted_iota(jnp.int32, (z.rows, 1), 0)
    block = steps(row, z.RP, z.local)
    place = row - block * z.RP
    both = steps(place, CAP, z.V + 1)
    slot = place - both * CAP
    fold = steps(both, z.each, z.folds)
    expert = both - fold * z.each
    plane = block
    if z.relative:
        plane = block + plane_ref[0]
        plane = jnp.where(plane >= z.local, plane - z.local, plane)
    name = jnp.where(place < z.R, plane * z.exp_dev + group * z.each + expert, -1)
    hits = [ids[k : k + 1, :] == name for k in range(ids.shape[0])]
    named = hits[0].astype(F32)
    for hit in hits[1:]:
        named = named + hit.astype(F32)
    t0 = lax.broadcasted_iota(jnp.int32, (z.tok, z.tok), 0)
    t1 = lax.broadcasted_iota(jnp.int32, (z.tok, z.tok), 1)
    before = jnp.where(t0 < t1, 1.0, 0.0).astype(BF16)
    rank = jnp.dot(named.astype(BF16), before, preferred_element_type=F32)
    here = rank == slot.astype(F32)
    return named, here, hits, fold


def gather_kernel(z, plane_ref, ids_ref, tokens_ref, *refs):
    outs, (names_ref, stack_ref, sem) = refs[:-3], refs[-3:]
    moves = [pltpu.make_async_copy(ids_ref, names_ref, sem.at[0])]
    for q in range(z.folds):
        src = tokens_ref.at[:, pl.ds(q * z.dc, z.dc)]
        moves.append(pltpu.make_async_copy(src, stack_ref.at[pl.ds(q * z.tok, z.tok)], sem.at[1 + q]))
    for move in moves:
        move.start()
    moves[0].wait()
    picks = []
    for g in range(z.groups):
        named, here, _, fold = slots(z, g, plane_ref, names_ref[...])
        pick = jnp.where(here, named, 0.0)
        picks.append(jnp.concatenate([jnp.where(fold == q, pick, 0.0) for q in range(z.folds)], axis=1).astype(BF16))
    for move in moves[1:]:
        move.wait()
    tile = tile_of(z.dc)

    def step(i, carry):
        cols = pl.ds(pl.multiple_of(i * tile, tile), tile)
        for g in range(z.groups):
            got = jnp.dot(picks[g], stack_ref[:, cols], preferred_element_type=F32).astype(BF16)
            for s in range(z.local):
                value = got[s * z.RP : s * z.RP + z.R]
                if not z.relative:
                    outs[g][s, :, cols] = value
                elif s == 0:
                    outs[0][g, :, cols] = value
                else:
                    outs[1 + g * (z.local - 1) + s - 1][0, :, cols] = value
        return carry

    lax.fori_loop(0, z.dc // tile, step, 0)


def gather_rows(z, plane, ids, tokens):
    if z.relative:
        shapes = [(z.groups, z.R, z.dc)] + [(1, z.R, z.dc)] * (z.groups * (z.local - 1))
    else:
        shapes = [(z.local, z.R, z.dc)] * z.groups
    outs = pl.pallas_call(
        functools.partial(gather_kernel, z),
        out_shape=[jax.ShapeDtypeStruct(s, BF16) for s in shapes],
        in_specs=[pl.BlockSpec(memory_space=pltpu.SMEM)] + [in_hbm()] * 2,
        out_specs=[in_vmem()] * len(shapes),
        scratch_shapes=[
            pltpu.VMEM((ids.shape[1], z.tok), jnp.int32),
            pltpu.VMEM((z.folds * z.tok, z.dc), BF16),
            pltpu.SemaphoreType.DMA((1 + z.folds,)),
        ],
        compiler_params=params(40),
        name="gather_rows",
    )(plane, ids.T, tokens)
    outs = list(outs)
    own = outs.pop(0) if z.relative else None
    each = z.local - 1 if z.relative else 1
    return own, [outs[i * each : (i + 1) * each] for i in range(z.groups)]


def weight_kernel(z, plane_ref, ids_ref, gates_ref, out_ref):
    gates = gates_ref[...]
    size = z.folds * z.tok
    for g in range(z.groups):
        _, here, hits, fold = slots(z, g, plane_ref, ids_ref[...])
        weight = jnp.zeros((z.rows, z.tok), F32)
        for k, hit in enumerate(hits):
            weight = weight + jnp.where(hit & here, gates[k : k + 1, :], 0.0)
        for q in range(z.folds):
            mine = jnp.where(fold == q, weight, 0.0).T
            high = mine.astype(BF16)
            out_ref[g, q * z.tok : (q + 1) * z.tok, :] = high
            out_ref[g, size + q * z.tok : size + (q + 1) * z.tok, :] = (mine - high.astype(F32)).astype(BF16)


def combine_weights(z, plane, ids, gates):
    return pl.pallas_call(
        functools.partial(weight_kernel, z),
        out_shape=jax.ShapeDtypeStruct((z.groups, 2 * z.folds * z.tok, z.rows), BF16),
        in_specs=[pl.BlockSpec(memory_space=pltpu.SMEM)] + [in_vmem()] * 2,
        out_specs=in_vmem(),
        compiler_params=params(40),
        name="combine_weights",
    )(plane, ids.T, gates.T)


def expert_kernel(z, group, places, order, *refs):
    pieces = refs[: len(places)]
    regroup_ref, ungroup_ref, wg_ref, wu_ref, wd_ref = refs[len(places) : len(places) + 5]
    outs = refs[len(places) + 5 : len(places) + 5 + len(order)]
    piece_ref, gate_ref, up_ref, down_ref, rows_ref, grouped_ref, hidden_ref, psem, wsem = refs[
        len(places) + 5 + len(order) :
    ]
    moves, at = [], 0
    for i, (ref, where) in enumerate(zip(pieces, places)):
        moves.append(pltpu.make_async_copy(ref, piece_ref.at[pl.ds(at, len(where))], psem.at[i]))
        moves[-1].start()
        at += len(where)
    loads = []
    for j in range(z.each):
        e = group * z.each + j
        for i, (src, dst) in enumerate(((wg_ref, gate_ref), (wu_ref, up_ref), (wd_ref, down_ref))):
            loads.append(pltpu.make_async_copy(src.at[e], dst.at[j], wsem.at[3 * j + i]))
    for i in [k for k in range(3 * z.each) if k % 3 < 2] + [k for k in range(3 * z.each) if k % 3 == 2]:
        loads[i].start()

    if z.RP > z.R:
        rows_ref[...] = jnp.zeros_like(rows_ref)
    at = 0
    for move, where in zip(moves, places):
        move.wait()
        for m, block in where:
            rows_ref[m, block * z.RP : block * z.RP + z.R, :] = piece_ref[at]
            at += 1
    tile = tile_of(z.dc)

    def step(i, carry):
        cols = pl.ds(pl.multiple_of(i * tile, tile), tile)
        for m in range(z.node):
            got = jnp.dot(regroup_ref[...], rows_ref[m, :, cols], preferred_element_type=F32).astype(BF16)
            got = got.reshape(z.V, z.MP, tile)
            for q in range(z.folds):
                there = pl.ds(pl.multiple_of(q * z.dc + i * tile, tile), tile)
                grouped_ref[:, m * z.MP : (m + 1) * z.MP, there] = got[q * z.each : (q + 1) * z.each]
        return carry

    lax.fori_loop(0, z.dc // tile, step, 0)

    for j in range(z.each):
        loads[3 * j].wait()
        gate = jnp.dot(grouped_ref[j], gate_ref[j], preferred_element_type=F32)
        loads[3 * j + 1].wait()
        up = jnp.dot(grouped_ref[j], up_ref[j], preferred_element_type=F32)
        hidden_ref[j] = (gate / (1.0 + jnp.exp(-gate)) * up).astype(BF16)

    for j in range(z.each):
        loads[3 * j + 2].wait()
        for q in range(z.folds):
            there = slice(q * z.dc, (q + 1) * z.dc)
            got = jnp.dot(hidden_ref[j], down_ref[j, :, there], preferred_element_type=F32)
            grouped_ref[j, :, there] = got.astype(BF16)

    def back(i, carry):
        cols = pl.ds(pl.multiple_of(i * tile, tile), tile)
        for out, ms in zip(outs, order):
            for k, m in enumerate(ms):
                held = []
                for q in range(z.folds):
                    there = pl.ds(pl.multiple_of(q * z.dc + i * tile, tile), tile)
                    held.append(grouped_ref[:, m * z.MP : (m + 1) * z.MP, there].reshape(z.each * z.MP, tile))
                got = jnp.dot(ungroup_ref[...], concat(*held), preferred_element_type=F32).astype(BF16)
                for s in range(z.local):
                    out[k * z.local + s, :, cols] = got[s * z.RP : s * z.RP + z.R]
        return carry

    lax.fori_loop(0, z.dc // tile, back, 0)


def expert_group(z, group, pieces, regroup, ungroup, w_gate, w_up, w_down, order):
    pieces, places = zip(*pieces)
    shapes = [jax.ShapeDtypeStruct((len(ms) * z.local, z.R, z.dc), BF16) for ms in order]
    scratch = [
        ((z.node * z.local, z.R, z.dc), BF16),
        ((z.each, z.width, z.hidden), BF16),
        ((z.each, z.width, z.hidden), BF16),
        ((z.each, z.hidden, z.width), BF16),
        ((z.node, z.rows, z.dc), BF16),
        ((z.each, z.node * z.MP, z.width), BF16),
        ((z.each, z.node * z.MP, z.hidden), BF16),
    ]
    return pl.pallas_call(
        functools.partial(expert_kernel, z, group, places, order),
        out_shape=shapes,
        in_specs=[in_hbm()] * len(pieces) + [in_vmem()] * 2 + [in_hbm()] * 3,
        out_specs=[in_vmem()] * len(shapes),
        scratch_shapes=[pltpu.VMEM(s, t) for s, t in scratch]
        + [pltpu.SemaphoreType.DMA((len(pieces),)), pltpu.SemaphoreType.DMA((3 * z.each,))],
        compiler_params=params(48 if z.relative else 60),
        cost_estimate=pl.CostEstimate(
            flops=6 * z.each * z.node * z.MP * z.width * z.hidden,
            bytes_accessed=6 * z.each * z.width * z.hidden,
            transcendentals=0,
        ),
        name="expert_group",
    )(*pieces, regroup, ungroup, w_gate, w_up, w_down)


def add_kernel(cuts, a_ref, b_ref, *outs):
    for out, (lo, hi) in zip(outs, cuts):
        out[...] = (a_ref[lo:hi].astype(F32) + b_ref[lo:hi].astype(F32)).astype(BF16)


def add_cut(a, b, cuts):
    return pl.pallas_call(
        functools.partial(add_kernel, cuts),
        out_shape=[jax.ShapeDtypeStruct((hi - lo,) + a.shape[1:], BF16) for lo, hi in cuts],
        in_specs=[in_vmem()] * 2,
        out_specs=[in_vmem()] * len(cuts),
        compiler_params=params(32),
        cost_estimate=pl.CostEstimate(flops=a.size, bytes_accessed=6 * a.size, transcendentals=0),
        name="add_cut",
    )(a, b)


def combine_kernel(z, group, counts, last, weight_ref, *refs):
    pieces = refs[: len(counts)]
    refs = refs[len(counts) :]
    if group > 0:
        before_ref = refs[0]
        refs = refs[1:]
    out_ref, rows_ref = refs
    if z.RP > z.R:
        rows_ref[...] = jnp.zeros_like(rows_ref)
    at = 0
    for ref, count in zip(pieces, counts):
        for i in range(count):
            rows_ref[at * z.RP : at * z.RP + z.R, :] = ref[i]
            at += 1
    size = z.folds * z.tok
    tile = tile_of(z.dc)
    for i in range(z.dc // tile):
        cols = slice(i * tile, (i + 1) * tile)
        terms = jnp.dot(weight_ref[group], rows_ref[:, cols], preferred_element_type=F32)
        total = terms[:size] + terms[size:]
        if group > 0:
            total = total + before_ref[:, cols]
        if last:
            for q in range(z.folds):
                there = slice(q * z.dc + i * tile, q * z.dc + (i + 1) * tile)
                out_ref[:, there] = total[q * z.tok : (q + 1) * z.tok].astype(BF16)
        else:
            out_ref[:, cols] = total


def combine_group(z, group, weight, pieces, before):
    last = group == z.groups - 1
    shape = jax.ShapeDtypeStruct((z.tok, z.width), BF16) if last else jax.ShapeDtypeStruct((z.folds * z.tok, z.dc), F32)
    extra = [] if group == 0 else [before]
    return pl.pallas_call(
        functools.partial(combine_kernel, z, group, [p.shape[0] for p in pieces], last),
        out_shape=shape,
        in_specs=[in_vmem()] * (1 + len(pieces) + len(extra)),
        out_specs=in_vmem(),
        scratch_shapes=[pltpu.VMEM((z.rows, z.dc), BF16)],
        compiler_params=params(32),
        name="combine_group",
    )(weight, *pieces, *extra)


def swap(a, mask, count):
    return lax.ppermute(a, "node", [(i, i ^ mask) for i in range(count)])


def shift(a, by, count):
    return lax.ppermute(a, "local", [(i, (i + by) % count) for i in range(count)])


def concat(*arrays):
    return jnp.concatenate(arrays, axis=0)


def per_device(tokens, expert_ids, gate_weights, w_gate, w_up, w_down):
    local_count, node_count = lax.axis_size("local"), lax.axis_size("node")
    z = Sizes(tokens, w_gate, local_count, node_count)
    plane = lax.axis_index("local").astype(jnp.int32).reshape(1)
    regroup = z.regroup()
    matrices = jnp.asarray(regroup, BF16), jnp.asarray(regroup.T, BF16)
    own, sent = gather_rows(z, plane, expert_ids, tokens)
    weight = combine_weights(z, plane, expert_ids, gate_weights)
    route = by_distance if z.relative else by_plane
    return route(z, weight, own, sent, matrices, (w_gate, w_up, w_down))


def by_distance(z, weight, own, sent, matrices, weights):
    count, blocks = z.local, range(1, z.local)
    order = sorted(blocks, key=lambda s: -min(s, count - s))
    done, result = [], None

    def recent():
        return done[-WINDOW - 2 : len(done) - WINDOW + 1] if len(done) >= WINDOW else []

    far = swap(own, 2, 4)
    came, stacks, across = {}, [], []

    def bring(*after):
        g = len(stacks)
        for s in order:
            came[g, s] = shift(tie(sent[g][s - 1], *recent(), *after), s, count)
            done.append(came[g, s])
        stacks.append(concat(*[came[g, s] for s in blocks]))
        across.append(swap(stacks[g], 2, 4))

    def pair_up(g, *after):
        a = tie(across[g], *after)
        pair = concat(own[g : g + 1], stacks[g], far[g : g + 1], a)
        return pair, swap(pair, 1, 4)

    def arrived(g, some):
        return [came[g, s] for s in some if (g, s) in came]

    for _ in range(min(AHEAD, z.groups)):
        bring()
    pair, beside = pair_up(0, *arrived(1, blocks))
    while len(stacks) < z.groups:
        bring(beside)
    keep, away, summed, parts, back = [], [], [], [], []

    def bring_back():
        k = len(parts)
        parts.append(add_cut(keep[k], summed[k], [(s, s + 1) for s in range(count)]))
        back.append({})
        for s in order:
            back[k][s] = shift(tie(parts[k][s], *recent()), -s, count)
            done.append(back[k][s])

    for g in range(z.groups):
        before = stacks[g + 2 : g + 3] + away[-1:] + list(parts[-1] if parts else ())
        pieces = [(tie(pair, *before), [(m, s) for m in (0, 2) for s in range(count)])]
        pieces.append((beside, [(m, s) for m in (1, 3) for s in range(count)]))
        send, kept = expert_group(z, g, pieces, *matrices, *weights, [[1, 3], [0, 2]])
        if g + 1 < z.groups:
            pair, beside = pair_up(g + 1, send)
        beside_it = across[g + 1 : g + 3] if g == 0 else across[g + 2 : g + 3]
        beside_it += [back[-1][s] for s in order] if back else []
        if g >= LAG:
            beside_it.append(summed[g - LAG])
            bring_back()
        got = swap(tie(send, *beside_it), 1, 4)
        k, a = add_cut(kept, got, [(0, count), (count, 2 * count)])
        keep.append(k)
        away.append(a)
        summed.append(swap(a, 2, 4))
    while len(parts) < z.groups:
        bring_back()
    for g in range(z.groups):
        result = combine_group(z, g, weight, [parts[g][0]] + [back[g][s] for s in blocks], result)
    return result


def spread(a, masks, count):
    held = {0: a}
    for mask in reversed(masks):
        for m in list(held):
            held[m | mask] = swap(held[m], mask, count)
    return held


def by_plane(z, weight, own, sent, matrices, weights):
    count, masks, result = z.local, [], None
    while 1 << len(masks) < z.node:
        masks.append(1 << len(masks))
    for g in range(z.groups):
        held = spread(lax.all_to_all(sent[g][0], "local", 0, 0, tiled=True), masks, z.node)
        pieces = [(held[m], [(m, s) for s in range(count)]) for m in range(z.node)]
        rows = expert_group(z, g, pieces, *matrices, *weights, [[m] for m in range(z.node)])
        rows = dict(enumerate(rows))
        for mask in masks:
            for m in [m for m in rows if not m & mask]:
                (rows[m],) = add_cut(rows[m], swap(rows.pop(m | mask), mask, z.node), [(0, count)])
        back = lax.all_to_all(rows[0], "local", 0, 0, tiled=True)
        result = combine_group(z, g, weight, [back], result)
    return result


def solution(mesh):
    return jax.shard_map(
        per_device,
        mesh=mesh,
        in_specs=(
            P(("parts", "node", "local"), None),
            P(("parts", "node", "local"), None),
            P(("parts", "node", "local"), None),
            P("local", None, "node"),
            P("local", None, "node"),
            P("local", "node", None),
        ),
        out_specs=P(("parts", "node", "local"), None),
        check_vma=False,
    )
```

```python
import functools
import math

import jax
import jax.numpy as jnp
import numpy as np
from jax import lax
from jax.experimental import pallas as pl
from jax.experimental.pallas import tpu as pltpu
from jax.sharding import PartitionSpec as P

CAP = 5
GROUPS = 4
WINDOW = 3
AHEAD = 3
LAG = 2
MIB = 1024 * 1024
F32, BF16 = jnp.float32, jnp.bfloat16


def pad16(n):
    return -(-n // 16) * 16


def params(mib):
    return pltpu.CompilerParams(vmem_limit_bytes=mib * MIB)


def in_vmem():
    return pl.BlockSpec(memory_space=pltpu.VMEM)


def in_hbm():
    return pl.BlockSpec(memory_space=pl.ANY)


def tie(a, *after):
    return lax.optimization_barrier((a,) + after)[0] if after else a


def tile_of(width):
    for t in (512, 256, 128):
        if width % t == 0:
            return t
    return width


class Sizes:
    def __init__(self, tokens, w_gate, local_count, node_count):
        self.tok, self.width = tokens.shape
        self.exp_dev = w_gate.shape[0]
        self.hidden = w_gate.shape[2]
        self.local = local_count
        self.node = node_count
        self.groups = math.gcd(self.exp_dev, GROUPS)
        self.each = self.exp_dev // self.groups
        self.folds = math.gcd(max(1, 8 // self.each), self.width // 128)
        self.dc = self.width // self.folds
        self.V = self.folds * self.each
        self.R = self.V * CAP
        self.RP = pad16(self.R)
        self.MP = pad16(self.local * CAP)
        self.rows = self.local * self.RP
        self.grouped = self.V * self.MP
        self.relative = local_count <= 4 and node_count == 4

    def regroup(self):
        m = np.zeros((self.grouped, self.rows), np.float32)
        for s in range(self.local):
            for j in range(self.V):
                for c in range(CAP):
                    m[j * self.MP + s * CAP + c, s * self.RP + j * CAP + c] = 1
        return m


def steps(a, width, count):
    total = jnp.zeros_like(a)
    for i in range(1, count):
        total = total + (a >= i * width).astype(jnp.int32)
    return total


def slots(z, group, plane_ref, ids):
    row = lax.broadcasted_iota(jnp.int32, (z.rows, 1), 0)
    block = steps(row, z.RP, z.local)
    place = row - block * z.RP
    both = steps(place, CAP, z.V + 1)
    slot = place - both * CAP
    fold = steps(both, z.each, z.folds)
    expert = both - fold * z.each
    plane = block
    if z.relative:
        plane = block + plane_ref[0]
        plane = jnp.where(plane >= z.local, plane - z.local, plane)
    name = jnp.where(place < z.R, plane * z.exp_dev + group * z.each + expert, -1)
    hits = [ids[k : k + 1, :] == name for k in range(ids.shape[0])]
    named = hits[0].astype(F32)
    for hit in hits[1:]:
        named = named + hit.astype(F32)
    t0 = lax.broadcasted_iota(jnp.int32, (z.tok, z.tok), 0)
    t1 = lax.broadcasted_iota(jnp.int32, (z.tok, z.tok), 1)
    before = jnp.where(t0 < t1, 1.0, 0.0).astype(BF16)
    rank = jnp.dot(named.astype(BF16), before, preferred_element_type=F32)
    here = rank == slot.astype(F32)
    return named, here, hits, fold


def gather_kernel(z, plane_ref, ids_ref, tokens_ref, *refs):
    outs, (names_ref, stack_ref, sem) = refs[:-3], refs[-3:]
    moves = [pltpu.make_async_copy(ids_ref, names_ref, sem.at[0])]
    for q in range(z.folds):
        src = tokens_ref.at[:, pl.ds(q * z.dc, z.dc)]
        moves.append(pltpu.make_async_copy(src, stack_ref.at[pl.ds(q * z.tok, z.tok)], sem.at[1 + q]))
    for move in moves:
        move.start()
    moves[0].wait()
    picks = []
    for g in range(z.groups):
        named, here, _, fold = slots(z, g, plane_ref, names_ref[...])
        pick = jnp.where(here, named, 0.0)
        picks.append(jnp.concatenate([jnp.where(fold == q, pick, 0.0) for q in range(z.folds)], axis=1).astype(BF16))
    for move in moves[1:]:
        move.wait()
    tile = tile_of(z.dc)

    def step(i, carry):
        cols = pl.ds(pl.multiple_of(i * tile, tile), tile)
        for g in range(z.groups):
            got = jnp.dot(picks[g], stack_ref[:, cols], preferred_element_type=F32).astype(BF16)
            for s in range(z.local):
                value = got[s * z.RP : s * z.RP + z.R]
                if not z.relative:
                    outs[g][s, :, cols] = value
                elif s == 0:
                    outs[0][g, :, cols] = value
                else:
                    outs[1 + g * (z.local - 1) + s - 1][0, :, cols] = value
        return carry

    lax.fori_loop(0, z.dc // tile, step, 0)


def gather_rows(z, plane, ids, tokens):
    if z.relative:
        shapes = [(z.groups, z.R, z.dc)] + [(1, z.R, z.dc)] * (z.groups * (z.local - 1))
    else:
        shapes = [(z.local, z.R, z.dc)] * z.groups
    outs = pl.pallas_call(
        functools.partial(gather_kernel, z),
        out_shape=[jax.ShapeDtypeStruct(s, BF16) for s in shapes],
        in_specs=[pl.BlockSpec(memory_space=pltpu.SMEM)] + [in_hbm()] * 2,
        out_specs=[in_vmem()] * len(shapes),
        scratch_shapes=[
            pltpu.VMEM((ids.shape[1], z.tok), jnp.int32),
            pltpu.VMEM((z.folds * z.tok, z.dc), BF16),
            pltpu.SemaphoreType.DMA((1 + z.folds,)),
        ],
        compiler_params=params(40),
        name="gather_rows",
    )(plane, ids.T, tokens)
    outs = list(outs)
    own = outs.pop(0) if z.relative else None
    each = z.local - 1 if z.relative else 1
    return own, [outs[i * each : (i + 1) * each] for i in range(z.groups)]


def weight_kernel(z, plane_ref, ids_ref, gates_ref, out_ref):
    gates = gates_ref[...]
    size = z.folds * z.tok
    for g in range(z.groups):
        _, here, hits, fold = slots(z, g, plane_ref, ids_ref[...])
        weight = jnp.zeros((z.rows, z.tok), F32)
        for k, hit in enumerate(hits):
            weight = weight + jnp.where(hit & here, gates[k : k + 1, :], 0.0)
        for q in range(z.folds):
            mine = jnp.where(fold == q, weight, 0.0).T
            high = mine.astype(BF16)
            out_ref[g, q * z.tok : (q + 1) * z.tok, :] = high
            out_ref[g, size + q * z.tok : size + (q + 1) * z.tok, :] = (mine - high.astype(F32)).astype(BF16)


def combine_weights(z, plane, ids, gates):
    return pl.pallas_call(
        functools.partial(weight_kernel, z),
        out_shape=jax.ShapeDtypeStruct((z.groups, 2 * z.folds * z.tok, z.rows), BF16),
        in_specs=[pl.BlockSpec(memory_space=pltpu.SMEM)] + [in_vmem()] * 2,
        out_specs=in_vmem(),
        compiler_params=params(40),
        name="combine_weights",
    )(plane, ids.T, gates.T)


def expert_kernel(z, group, places, order, *refs):
    pieces = refs[: len(places)]
    regroup_ref, ungroup_ref, wg_ref, wu_ref, wd_ref = refs[len(places) : len(places) + 5]
    outs = refs[len(places) + 5 : len(places) + 5 + len(order)]
    piece_ref, gate_ref, up_ref, down_ref, rows_ref, grouped_ref, hidden_ref, psem, wsem = refs[
        len(places) + 5 + len(order) :
    ]
    moves, at = [], 0
    for i, (ref, where) in enumerate(zip(pieces, places)):
        moves.append(pltpu.make_async_copy(ref, piece_ref.at[pl.ds(at, len(where))], psem.at[i]))
        moves[-1].start()
        at += len(where)
    loads = []
    for j in range(z.each):
        e = group * z.each + j
        for i, (src, dst) in enumerate(((wg_ref, gate_ref), (wu_ref, up_ref), (wd_ref, down_ref))):
            loads.append(pltpu.make_async_copy(src.at[e], dst.at[j], wsem.at[3 * j + i]))
    for i in [k for k in range(3 * z.each) if k % 3 < 2] + [k for k in range(3 * z.each) if k % 3 == 2]:
        loads[i].start()

    if z.RP > z.R:
        rows_ref[...] = jnp.zeros_like(rows_ref)
    at = 0
    for move, where in zip(moves, places):
        move.wait()
        for m, block in where:
            rows_ref[m, block * z.RP : block * z.RP + z.R, :] = piece_ref[at]
            at += 1
    tile = tile_of(z.dc)

    def step(i, carry):
        cols = pl.ds(pl.multiple_of(i * tile, tile), tile)
        for m in range(z.node):
            got = jnp.dot(regroup_ref[...], rows_ref[m, :, cols], preferred_element_type=F32).astype(BF16)
            got = got.reshape(z.V, z.MP, tile)
            for q in range(z.folds):
                there = pl.ds(pl.multiple_of(q * z.dc + i * tile, tile), tile)
                grouped_ref[:, m * z.MP : (m + 1) * z.MP, there] = got[q * z.each : (q + 1) * z.each]
        return carry

    lax.fori_loop(0, z.dc // tile, step, 0, unroll=z.relative)

    for j in range(z.each):
        loads[3 * j].wait()
        gate = jnp.dot(grouped_ref[j], gate_ref[j], preferred_element_type=F32)
        loads[3 * j + 1].wait()
        up = jnp.dot(grouped_ref[j], up_ref[j], preferred_element_type=F32)
        hidden_ref[j] = (gate / (1.0 + jnp.exp(-gate)) * up).astype(BF16)

    for j in range(z.each):
        loads[3 * j + 2].wait()
        for q in range(z.folds):
            there = slice(q * z.dc, (q + 1) * z.dc)
            got = jnp.dot(hidden_ref[j], down_ref[j, :, there], preferred_element_type=F32)
            grouped_ref[j, :, there] = got.astype(BF16)

    def back(i, carry):
        cols = pl.ds(pl.multiple_of(i * tile, tile), tile)
        for out, ms in zip(outs, order):
            for k, m in enumerate(ms):
                held = []
                for q in range(z.folds):
                    there = pl.ds(pl.multiple_of(q * z.dc + i * tile, tile), tile)
                    held.append(grouped_ref[:, m * z.MP : (m + 1) * z.MP, there].reshape(z.each * z.MP, tile))
                got = jnp.dot(ungroup_ref[...], concat(*held), preferred_element_type=F32).astype(BF16)
                for s in range(z.local):
                    out[k * z.local + s, :, cols] = got[s * z.RP : s * z.RP + z.R]
        return carry

    lax.fori_loop(0, z.dc // tile, back, 0, unroll=z.relative)


def expert_group(z, group, pieces, regroup, ungroup, w_gate, w_up, w_down, order):
    pieces, places = zip(*pieces)
    shapes = [jax.ShapeDtypeStruct((len(ms) * z.local, z.R, z.dc), BF16) for ms in order]
    scratch = [
        ((z.node * z.local, z.R, z.dc), BF16),
        ((z.each, z.width, z.hidden), BF16),
        ((z.each, z.width, z.hidden), BF16),
        ((z.each, z.hidden, z.width), BF16),
        ((z.node, z.rows, z.dc), BF16),
        ((z.each, z.node * z.MP, z.width), BF16),
        ((z.each, z.node * z.MP, z.hidden), BF16),
    ]
    return pl.pallas_call(
        functools.partial(expert_kernel, z, group, places, order),
        out_shape=shapes,
        in_specs=[in_hbm()] * len(pieces) + [in_vmem()] * 2 + [in_hbm()] * 3,
        out_specs=[in_vmem()] * len(shapes),
        scratch_shapes=[pltpu.VMEM(s, t) for s, t in scratch]
        + [pltpu.SemaphoreType.DMA((len(pieces),)), pltpu.SemaphoreType.DMA((3 * z.each,))],
        compiler_params=params(48 if z.relative else 60),
        cost_estimate=pl.CostEstimate(
            flops=6 * z.each * z.node * z.MP * z.width * z.hidden,
            bytes_accessed=6 * z.each * z.width * z.hidden,
            transcendentals=0,
        ),
        name="expert_group",
    )(*pieces, regroup, ungroup, w_gate, w_up, w_down)


def add_kernel(cuts, a_ref, b_ref, *outs):
    for out, (lo, hi) in zip(outs, cuts):
        out[...] = (a_ref[lo:hi].astype(F32) + b_ref[lo:hi].astype(F32)).astype(BF16)


def add_cut(a, b, cuts):
    return pl.pallas_call(
        functools.partial(add_kernel, cuts),
        out_shape=[jax.ShapeDtypeStruct((hi - lo,) + a.shape[1:], BF16) for lo, hi in cuts],
        in_specs=[in_vmem()] * 2,
        out_specs=[in_vmem()] * len(cuts),
        compiler_params=params(32),
        cost_estimate=pl.CostEstimate(flops=a.size, bytes_accessed=6 * a.size, transcendentals=0),
        name="add_cut",
    )(a, b)


def combine_kernel(z, group, counts, last, weight_ref, *refs):
    pieces = refs[: len(counts)]
    refs = refs[len(counts) :]
    if group > 0:
        before_ref = refs[0]
        refs = refs[1:]
    out_ref, rows_ref = refs
    if z.RP > z.R:
        rows_ref[...] = jnp.zeros_like(rows_ref)
    at = 0
    for ref, count in zip(pieces, counts):
        for i in range(count):
            rows_ref[at * z.RP : at * z.RP + z.R, :] = ref[i]
            at += 1
    size = z.folds * z.tok
    tile = tile_of(z.dc)
    for i in range(z.dc // tile):
        cols = slice(i * tile, (i + 1) * tile)
        terms = jnp.dot(weight_ref[group], rows_ref[:, cols], preferred_element_type=F32)
        total = terms[:size] + terms[size:]
        if group > 0:
            total = total + before_ref[:, cols]
        if last:
            for q in range(z.folds):
                there = slice(q * z.dc + i * tile, q * z.dc + (i + 1) * tile)
                out_ref[:, there] = total[q * z.tok : (q + 1) * z.tok].astype(BF16)
        else:
            out_ref[:, cols] = total


def combine_group(z, group, weight, pieces, before):
    last = group == z.groups - 1
    shape = jax.ShapeDtypeStruct((z.tok, z.width), BF16) if last else jax.ShapeDtypeStruct((z.folds * z.tok, z.dc), F32)
    extra = [] if group == 0 else [before]
    return pl.pallas_call(
        functools.partial(combine_kernel, z, group, [p.shape[0] for p in pieces], last),
        out_shape=shape,
        in_specs=[in_vmem()] * (1 + len(pieces) + len(extra)),
        out_specs=in_vmem(),
        scratch_shapes=[pltpu.VMEM((z.rows, z.dc), BF16)],
        compiler_params=params(32),
        name="combine_group",
    )(weight, *pieces, *extra)


def swap(a, mask, count):
    return lax.ppermute(a, "node", [(i, i ^ mask) for i in range(count)])


def shift(a, by, count):
    return lax.ppermute(a, "local", [(i, (i + by) % count) for i in range(count)])


def concat(*arrays):
    return jnp.concatenate(arrays, axis=0)


def per_device(tokens, expert_ids, gate_weights, w_gate, w_up, w_down):
    local_count, node_count = lax.axis_size("local"), lax.axis_size("node")
    z = Sizes(tokens, w_gate, local_count, node_count)
    plane = lax.axis_index("local").astype(jnp.int32).reshape(1)
    regroup = z.regroup()
    matrices = jnp.asarray(regroup, BF16), jnp.asarray(regroup.T, BF16)
    own, sent = gather_rows(z, plane, expert_ids, tokens)
    weight = combine_weights(z, plane, expert_ids, gate_weights)
    route = by_distance if z.relative else by_plane
    return route(z, weight, own, sent, matrices, (w_gate, w_up, w_down))


def by_distance(z, weight, own, sent, matrices, weights):
    count, blocks = z.local, range(1, z.local)
    order = sorted(blocks, key=lambda s: -min(s, count - s))
    done, result = [], None

    def recent():
        return done[-WINDOW - 2 : len(done) - WINDOW + 1] if len(done) >= WINDOW else []

    far = swap(own, 2, 4)
    came, stacks, across = {}, [], []

    def bring(*after):
        g = len(stacks)
        for s in order:
            came[g, s] = shift(tie(sent[g][s - 1], *recent(), *after), s, count)
            done.append(came[g, s])
        stacks.append(concat(*[came[g, s] for s in blocks]))
        across.append(swap(stacks[g], 2, 4))

    def pair_up(g, *after):
        a = tie(across[g], *after)
        pair = concat(own[g : g + 1], stacks[g], far[g : g + 1], a)
        return pair, swap(pair, 1, 4)

    def arrived(g, some):
        return [came[g, s] for s in some if (g, s) in came]

    for _ in range(min(AHEAD, z.groups)):
        bring()
    pair, beside = pair_up(0, *arrived(1, blocks))
    while len(stacks) < z.groups:
        bring(beside)
    keep, away, summed, parts, back = [], [], [], [], []

    def bring_back():
        k = len(parts)
        parts.append(add_cut(keep[k], summed[k], [(s, s + 1) for s in range(count)]))
        back.append({})
        for s in order:
            back[k][s] = shift(tie(parts[k][s], *recent()), -s, count)
            done.append(back[k][s])

    for g in range(z.groups):
        before = stacks[g + 2 : g + 3] + away[-1:] + list(parts[-1] if parts else ())
        pieces = [(tie(pair, *before), [(m, s) for m in (0, 2) for s in range(count)])]
        pieces.append((beside, [(m, s) for m in (1, 3) for s in range(count)]))
        send, kept = expert_group(z, g, pieces, *matrices, *weights, [[1, 3], [0, 2]])
        if g + 1 < z.groups:
            pair, beside = pair_up(g + 1, send)
        beside_it = across[g + 1 : g + 3] if g == 0 else across[g + 2 : g + 3]
        beside_it += [back[-1][s] for s in order] if back else []
        if g >= LAG:
            beside_it.append(summed[g - LAG])
            bring_back()
        got = swap(tie(send, *beside_it), 1, 4)
        k, a = add_cut(kept, got, [(0, count), (count, 2 * count)])
        keep.append(k)
        away.append(a)
        summed.append(swap(a, 2, 4))
    while len(parts) < z.groups:
        bring_back()
    for g in range(z.groups):
        result = combine_group(z, g, weight, [parts[g][0]] + [back[g][s] for s in blocks], result)
    return result


def spread(a, masks, count):
    held = {0: a}
    for mask in reversed(masks):
        for m in list(held):
            held[m | mask] = swap(held[m], mask, count)
    return held


def by_plane(z, weight, own, sent, matrices, weights):
    count, masks, result = z.local, [], None
    while 1 << len(masks) < z.node:
        masks.append(1 << len(masks))
    for g in range(z.groups):
        held = spread(lax.all_to_all(sent[g][0], "local", 0, 0, tiled=True), masks, z.node)
        pieces = [(held[m], [(m, s) for s in range(count)]) for m in range(z.node)]
        rows = expert_group(z, g, pieces, *matrices, *weights, [[m] for m in range(z.node)])
        rows = dict(enumerate(rows))
        for mask in masks:
            for m in [m for m in rows if not m & mask]:
                (rows[m],) = add_cut(rows[m], swap(rows.pop(m | mask), mask, z.node), [(0, count)])
        back = lax.all_to_all(rows[0], "local", 0, 0, tiled=True)
        result = combine_group(z, g, weight, [back], result)
    return result


def solution(mesh):
    return jax.shard_map(
        per_device,
        mesh=mesh,
        in_specs=(
            P(("parts", "node", "local"), None),
            P(("parts", "node", "local"), None),
            P(("parts", "node", "local"), None),
            P("local", None, "node"),
            P("local", None, "node"),
            P("local", "node", None),
        ),
        out_specs=P(("parts", "node", "local"), None),
        check_vma=False,
    )
```
